32 devices in a mesh: batch: 4 (over x, core), ctx: 4 (over z), head: 2 (over y).
Axes of the slice: x: 2, y: 2, z: 4, core: 2. Of those that a mesh axis runs over, the one named last changes fastest.
Arguments:
- queries: bfloat16 [2, 2048, 1536], P(None, ('batch', 'ctx'), 'head'), parts along dimension 1, may hold values from -6 to 6
- keyvals: bfloat16 [4, 2048, 1536], P(None, ('batch', 'ctx'), 'head'), parts along dimension 1, may hold values from -6 to 6
- w_out: bfloat16 [1536, 3072], P('head'), may hold values from -2.390625 to 2.390625
Outputs:
- output: bfloat16 [2048, 3072], P(('batch', 'ctx'), 'head'), parts along dimension 0
- output_tangent: bfloat16 [2048, 3072], P(('batch', 'ctx'), 'head'), parts along dimension 0
The draws below stay inside these ranges and needn't reach their ends.
There are 4 independent parts, one for each index of `batch`. The reference program is written for one: setup_inputs(seed, part) draws one part's arguments, and reference() takes and returns one part's arrays. A program takes and returns all parts, laid end to end along the dimension named above; an argument that names none is the same for every part. Nothing has to cross between parts.
All inputs are finite; a program needn't handle non-finite values.
Results may differ from the reference program's by a relative error of at most 0.01.
Values may be sent and summed in bfloat16 or wider, within the bound.
A program may use at most 64 MiB of HBM per device.

```python
import math
import jax
import jax.numpy as jnp
from jax import lax

D = 3072
HEADS = 12
HD = 128
RADIUS = 2
TOK_DEV = 128
SEQ = 512
N_CTX = 4


def base_values(key, shape):
    return jnp.clip(jax.random.normal(key, shape, jnp.float32), -6.0, 6.0)


def draw_queries(key, part):
    values = base_values(jax.random.fold_in(key, 1), (2, SEQ, HEADS * HD))
    return values.astype(jnp.bfloat16)


def draw_keyvals(key, part):
    values = base_values(jax.random.fold_in(key, 2), (4, SEQ, HEADS * HD))
    return values.astype(jnp.bfloat16)


def levels(stream_key, dims, cuts, least, top_value):
    def one(dim, parts):
        heights = jax.random.uniform(jax.random.fold_in(jax.random.fold_in(stream_key, 6), dim), (parts,), jnp.float32, least / len(cuts), top_value / len(cuts))
        return jnp.repeat(jnp.exp(heights), dims[dim] // parts).reshape((-1,) + (1,) * (len(dims) - dim - 1))

    factor_of = one(*cuts[0])
    for cut in cuts[1:]:
        factor_of = factor_of * one(*cut)
    return factor_of


def noise(key, shape, deviation, reach, cuts=(), held_as=jnp.bfloat16):
    entries = deviation * jax.random.normal(key, shape, jnp.float32)
    if cuts:
        entries = entries * levels(key, shape, cuts, -0.22, 0.18)
    return jnp.clip(entries, -reach, reach).astype(held_as)


def setup_inputs(seed: int = 0, part: int = 0) -> dict:
    key_of = jax.random.split(jax.random.key(seed), 4)
    own_keys = jax.random.split(jax.random.fold_in(key_of[3], part), 4)
    return {
        "queries": draw_queries(jax.random.fold_in(jax.random.fold_in(key_of[3], part), 71), part),
        "keyvals": draw_keyvals(jax.random.fold_in(jax.random.fold_in(key_of[3], part), 71), part),
        "w_out": noise(key_of[2], (HEADS * HD, D), 0.4, 2.390625, ((0, 2),)),
    }


def attend(query_pair, key_block, visible, w_out):
    row_count = query_pair.shape[1]
    key_count = key_block.shape[1]
    head_count = query_pair.shape[2] // HD
    score_scale = 1.0 / math.sqrt(HD)
    query_now = query_pair[0].reshape(row_count, head_count, HD).astype(jnp.float32)
    query_tan = query_pair[1].reshape(row_count, head_count, HD).astype(jnp.float32)
    key_now = key_block[0].reshape(key_count, head_count, HD).astype(jnp.float32)
    value_now = key_block[1].reshape(key_count, head_count, HD).astype(jnp.float32)
    key_tan = key_block[2].reshape(key_count, head_count, HD).astype(jnp.float32)
    value_tan = key_block[3].reshape(key_count, head_count, HD).astype(jnp.float32)
    scores = jnp.einsum('qhd,khd->hqk', query_now, key_now) * score_scale
    scores = jnp.where(visible[None, None, :], scores, -jnp.inf)
    row_max = lax.optimization_barrier(jnp.max(scores, axis=-1, keepdims=True))
    expo = jnp.exp(scores - row_max)
    prob_f = expo / lax.optimization_barrier(jnp.sum(expo, axis=-1, keepdims=True))
    tan_scores = (jnp.einsum('qhd,khd->hqk', query_tan, key_now) + jnp.einsum('qhd,khd->hqk', query_now, key_tan)) * score_scale
    weighted = prob_f * tan_scores
    tan_shift = lax.optimization_barrier(jnp.sum(weighted, axis=-1))
    prob_b = prob_f.astype(jnp.bfloat16).astype(jnp.float32)
    weight_b = weighted.astype(jnp.bfloat16).astype(jnp.float32)
    attended = jnp.einsum('hqk,khd->qhd', prob_b, value_now)
    att_tan = jnp.einsum('hqk,khd->qhd', weight_b, value_now) + jnp.einsum('hqk,khd->qhd', prob_b, value_tan) - jnp.transpose(tan_shift)[:, :, None] * attended
    att_flat = attended.reshape(row_count, head_count * HD).astype(jnp.bfloat16)
    tan_flat = att_tan.reshape(row_count, head_count * HD).astype(jnp.bfloat16)
    projected = jnp.dot(att_flat, w_out, preferred_element_type=jnp.float32)
    projected_tan = jnp.dot(tan_flat, w_out, preferred_element_type=jnp.float32)
    return (projected, projected_tan)

def reference(queries, keyvals, w_out):
    margin = RADIUS * TOK_DEV
    padded = jnp.pad(keyvals, ((0, 0), (margin, margin), (0, 0)))
    key_count = (2 * RADIUS + 1) * TOK_DEV
    offsets = jnp.arange(key_count, dtype=jnp.int32) // TOK_DEV - RADIUS

    def one_block(block):
        start = (block * TOK_DEV).astype(jnp.int32)
        query_pair = lax.dynamic_slice_in_dim(queries, start, TOK_DEV, 1)
        key_block = lax.dynamic_slice_in_dim(padded, start, key_count, 1)
        target = block + offsets
        visible = (target >= 0) & (target < N_CTX)
        return attend(query_pair, key_block, visible, w_out)
    projected, projected_tan = lax.map(one_block, jnp.arange(N_CTX, dtype=jnp.int32))
    output = projected.reshape(N_CTX * TOK_DEV, D).astype(jnp.bfloat16)
    output_tangent = projected_tan.reshape(N_CTX * TOK_DEV, D).astype(jnp.bfloat16)
    return (output, output_tangent)
```

```python
import functools
import math

import jax
import jax.numpy as jnp
from jax import lax
from jax.experimental import pallas as pl
from jax.experimental.pallas import tpu as pltpu
from jax.sharding import PartitionSpec as P

HD = 128
RADIUS = 2
AHEAD = 2
MESH = pl.DeviceIdType.MESH


def kernel(
    sizes, queries, keyvals, w_out, out, out_tan,
    q, kv, w, att, acc,
    q_sem, own_sem, w_sem, kv_send, kv_recv, att_send, att_recv,
    wy_send, wy_recv, wb_send, wb_recv,
):
    n_ctx, n_head, n_batch = sizes
    rows = queries.shape[1]
    width = queries.shape[2]
    heads = width // HD
    cols = out.shape[1]
    slots = min(n_ctx, 2 * RADIUS + 1)
    me = lax.axis_index("ctx")
    mine = lax.axis_index("head")
    b = lax.axis_index("batch")
    bits = [2, 1] if n_batch % 4 == 0 else [1] if n_batch % 2 == 0 else []
    piece = width // (1 << len(bits))

    def slot_of(tile, at):
        return tile if n_ctx <= 2 * RADIUS + 1 else tile - at + RADIUS

    def tile_rows(slot):
        return pl.ds(pl.multiple_of(slot * rows, rows), rows)

    def head_cols(h):
        return pl.ds(h * HD, HD)

    def w_rows(group, first, count):
        return pl.ds(pl.multiple_of(group * width + first, 64), count)

    def w_cols(group):
        return pl.ds(pl.multiple_of(group * cols, 128), cols)

    def sign(d):
        return 1 if d == 0 else -1

    def kv_copy(d, r, h):
        tile = me - sign(d) * (r - 1)
        to = me + sign(d)
        if r == 1:
            src = keyvals.at[:, :, head_cols(h)]
        else:
            src = kv.at[h, :, tile_rows(slot_of(tile, me)), :]
        return pltpu.make_async_remote_copy(
            src_ref=src,
            dst_ref=kv.at[h, :, tile_rows(slot_of(tile, to)), :],
            send_sem=kv_send.at[d, r - 1, h],
            recv_sem=kv_recv.at[d, r - 1, h],
            device_id={"ctx": to},
            device_id_type=MESH,
        )

    def kv_arrival(d, r, h):
        here = kv.at[h, :, tile_rows(slot_of(me - sign(d) * r, me)), :]
        return pltpu.make_async_remote_copy(
            src_ref=here, dst_ref=here,
            send_sem=kv_send.at[d, r - 1, h],
            recv_sem=kv_recv.at[d, r - 1, h],
            device_id={"ctx": me - sign(d)},
            device_id_type=MESH,
        )

    def sends(d, r):
        if d == 0:
            return (me - (r - 1) >= 0) & (me + 1 < n_ctx)
        return (me + (r - 1) < n_ctx) & (me - 1 >= 0)

    def gets(d, r):
        return me - r >= 0 if d == 0 else me + r < n_ctx

    def kv_start(r, h):
        for d in range(2):
            @pl.when(sends(d, r))
            def _():
                kv_copy(d, r, h).start()

    def kv_wait(r, h):
        for d in range(2):
            @pl.when(gets(d, r))
            def _():
                kv_arrival(d, r, h).wait_recv()

    def bit_of(bit):
        return lax.rem(b // bit, 2)

    def partner(bit):
        return b + bit - 2 * bit * bit_of(bit)

    number = 0
    for place, bit in enumerate(bits):
        number = number + bit_of(bit) * (1 << place)

    def wy_copy(d):
        peer = lax.rem(mine + d, n_head)
        return pltpu.make_async_remote_copy(
            src_ref=w_out.at[pl.ds(pl.multiple_of(number * piece, 64), piece), w_cols(peer)],
            dst_ref=w.at[w_rows(mine, number * piece, piece), :],
            send_sem=wy_send.at[d - 1],
            recv_sem=wy_recv.at[d - 1],
            device_id={"head": peer},
            device_id_type=MESH,
        )

    def wy_arrival(d):
        sender = lax.rem(mine + n_head - d, n_head)
        here = w.at[w_rows(sender, number * piece, piece), :]
        return pltpu.make_async_remote_copy(
            src_ref=here, dst_ref=here,
            send_sem=wy_send.at[d - 1], recv_sem=wy_recv.at[d - 1],
            device_id={"head": sender}, device_id_type=MESH,
        )

    def wb_copy(level, d, receive=False):
        sender = lax.rem(mine + n_head - d, n_head)
        block = piece << level
        index = number // (1 << level)
        if receive:
            index = index + 1 - 2 * lax.rem(index, 2)
        here = w.at[w_rows(sender, index * block, block), :]
        return pltpu.make_async_remote_copy(
            src_ref=here, dst_ref=here,
            send_sem=wb_send.at[level, d - 1], recv_sem=wb_recv.at[level, d - 1],
            device_id={"batch": partner(bits[level])}, device_id_type=MESH,
        )

    def w_step(stage):
        for d in range(1, n_head):
            if stage == 0:
                wy_arrival(d).wait_recv()
            else:
                wb_copy(stage - 1, d, receive=True).wait_recv()
            if stage < len(bits):
                wb_copy(stage, d).start()

    def att_copy(d, h):
        return pltpu.make_async_remote_copy(
            src_ref=att.at[mine, h], dst_ref=att.at[mine, h],
            send_sem=att_send.at[d - 1, h], recv_sem=att_recv.at[d - 1, h],
            device_id={"head": lax.rem(mine + d, n_head)}, device_id_type=MESH,
        )

    def att_arrival(d, h):
        sender = lax.rem(mine + n_head - d, n_head)
        return pltpu.make_async_remote_copy(
            src_ref=att.at[sender, h], dst_ref=att.at[sender, h],
            send_sem=att_send.at[d - 1, h], recv_sem=att_recv.at[d - 1, h],
            device_id={"head": sender}, device_id_type=MESH,
        )

    def q_load():
        return pltpu.make_async_copy(queries, q, q_sem)

    def own_load(h):
        return pltpu.make_async_copy(
            keyvals.at[:, :, head_cols(h)],
            kv.at[h, :, tile_rows(slot_of(me, me)), :],
            own_sem.at[h],
        )

    def w_load():
        return pltpu.make_async_copy(
            w_out.at[:, w_cols(mine)], w.at[w_rows(mine, 0, width), :], w_sem
        )

    barrier = pltpu.get_barrier_semaphore()
    for d in range(2):
        @pl.when(sends(d, 1))
        def _():
            pl.semaphore_signal(
                barrier, inc=1, device_id={"ctx": me + sign(d)}, device_id_type=MESH
            )
    for d in range(1, n_head):
        pl.semaphore_signal(
            barrier, inc=1, device_id={"head": lax.rem(mine + d, n_head)}, device_id_type=MESH
        )
    for bit in bits:
        pl.semaphore_signal(
            barrier, inc=1, device_id={"batch": partner(bit)}, device_id_type=MESH
        )
    q_load().start()
    for h in range(heads):
        own_load(h).start()
    w_load().start()
    base = slot_of(0, me)
    for slot in range(slots):
        tile = slot - base
        @pl.when((tile < 0) | (tile >= n_ctx) | (tile - me > RADIUS) | (me - tile > RADIUS))
        def _():
            kv[:, :, slot * rows:(slot + 1) * rows, :] = jnp.zeros(
                (heads, 4, rows, HD), jnp.bfloat16
            )
    near = jnp.where(me > 0, 1, 0) + jnp.where(me + 1 < n_ctx, 1, 0)
    pl.semaphore_wait(barrier, near + (n_head - 1 + len(bits)))

    for h in range(min(AHEAD, heads)):
        kv_start(1, h)
    for d in range(1, n_head):
        wy_copy(d).start()

    column_tile = lax.broadcasted_iota(jnp.int32, (1, slots * rows), 1) // rows - base
    visible = (
        (column_tile >= 0) & (column_tile < n_ctx)
        & (column_tile - me <= RADIUS) & (me - column_tile <= RADIUS)
    )
    scale = 1.0 / math.sqrt(HD)

    def attend(h):
        at = slice(h * HD, (h + 1) * HD)
        q_now, q_tan = q[0, :, at], q[1, :, at]
        lhs = jnp.concatenate(
            [
                jnp.concatenate([q_now, jnp.zeros_like(q_now)], axis=1),
                jnp.concatenate([q_tan, q_now], axis=1),
            ],
            axis=0,
        )
        keys = jnp.concatenate([kv[h, 0], kv[h, 2]], axis=1)
        values = jnp.concatenate([kv[h, 1], kv[h, 3]], axis=1)
        both = lax.dot_general(
            lhs, keys, (((1,), (1,)), ((), ())), preferred_element_type=jnp.float32
        )
        scores = jnp.where(visible, both[:rows], -jnp.inf)
        row_max = jnp.max(scores, axis=-1, keepdims=True)
        expo = jnp.exp2((scores - row_max) * (scale * math.log2(math.e)))
        prob = expo * (1.0 / jnp.sum(expo, axis=-1, keepdims=True))
        weighted = prob * (both[rows:] * scale)
        shift = jnp.sum(weighted, axis=-1, keepdims=True)
        left = jnp.concatenate([prob.astype(jnp.bfloat16), weighted.astype(jnp.bfloat16)], axis=0)
        mixed = jnp.dot(left, values, preferred_element_type=jnp.float32)
        attended = mixed[:rows, :HD]
        tangent = mixed[rows:, :HD] + mixed[:rows, HD:] - shift * attended
        att[mine, h, :rows] = attended.astype(jnp.bfloat16)
        att[mine, h, rows:] = tangent.astype(jnp.bfloat16)
        for d in range(1, n_head):
            att_copy(d, h).start()

    def project(group, first, count, fresh=False):
        left = jnp.concatenate([att[group, first + i] for i in range(count)], axis=1)
        part = jnp.dot(
            left, w[w_rows(group, first * HD, count * HD), :], preferred_element_type=jnp.float32
        )
        if fresh:
            acc[...] = part
        else:
            acc[...] += part

    pair = 2 if heads % 2 == 0 else 1

    def near_step(h):
        kv_wait(1, h)
        kv_start(2, h)
        if h + AHEAD < heads:
            kv_start(1, h + AHEAD)

    q_load().wait()
    near_step(0)
    stage = 0
    w_at = {heads // 2: 0, heads - 1: 1}
    for h in range(heads):
        if h + 1 < heads:
            near_step(h + 1)
        if h == 0:
            w_load().wait()
        own_load(h).wait()
        kv_wait(2, h)
        attend(h)
        if h in w_at and stage <= len(bits):
            w_step(stage)
            stage += 1
        if (h + 1) % pair == 0:
            project(mine, h + 1 - pair, pair, fresh=h + 1 == pair)
    while stage <= len(bits):
        w_step(stage)
        stage += 1
    for first in range(0, heads, pair):
        for d in range(1, n_head):
            for i in range(pair):
                att_arrival(d, first + i).wait_recv()
            project(lax.rem(mine + n_head - d, n_head), first, pair)
    out[...] = acc[:rows].astype(out.dtype)
    out_tan[...] = acc[rows:].astype(out_tan.dtype)

    for h in range(heads):
        for r in range(1, RADIUS + 1):
            for d in range(2):
                @pl.when(sends(d, r))
                def _():
                    kv_copy(d, r, h).wait_send()
        for d in range(1, n_head):
            att_copy(d, h).wait_send()
    for d in range(1, n_head):
        wy_copy(d).wait_send()
        for level in range(len(bits)):
            wb_copy(level, d).wait_send()


def per_device(sizes, queries, keyvals, w_out):
    n_ctx, n_head, n_batch = sizes
    rows, width = queries.shape[1], queries.shape[2]
    heads = width // HD
    cols = w_out.shape[1] // n_head
    slots = min(n_ctx, 2 * RADIUS + 1)
    dma = pltpu.SemaphoreType.DMA
    peers = max(n_head - 1, 1)
    return pl.pallas_call(
        functools.partial(kernel, sizes),
        out_shape=[jax.ShapeDtypeStruct((rows, cols), jnp.bfloat16)] * 2,
        in_specs=[pl.BlockSpec(memory_space=pl.ANY)] * 3,
        out_specs=[pl.BlockSpec(memory_space=pltpu.VMEM)] * 2,
        scratch_shapes=[
            pltpu.VMEM((2, rows, width), jnp.bfloat16),
            pltpu.VMEM((heads, 4, slots * rows, HD), jnp.bfloat16),
            pltpu.VMEM((n_head * width, cols), jnp.bfloat16),
            pltpu.VMEM((n_head, heads, 2 * rows, HD), jnp.bfloat16),
            pltpu.VMEM((2 * rows, cols), jnp.float32),
            dma, dma((heads,)), dma,
            dma((2, RADIUS, heads)), dma((2, RADIUS, heads)),
            dma((peers, heads)), dma((peers, heads)),
            dma((peers,)), dma((peers,)),
            dma((2, peers)), dma((2, peers)),
        ],
        compiler_params=pltpu.CompilerParams(
            collective_id=0, has_side_effects=True, vmem_limit_bytes=40 * 1024 * 1024
        ),
        cost_estimate=pl.CostEstimate(
            flops=2 * 2 * rows * n_head * width * cols,
            bytes_accessed=16 * rows * width + 2 * w_out.size,
            transcendentals=heads * rows * slots * rows,
        ),
    )(queries, keyvals, w_out)


def solution(mesh):
    sizes = (mesh.shape["ctx"], mesh.shape["head"], mesh.shape["batch"])
    in_specs = (
        P(None, ("batch", "ctx"), "head"),
        P(None, ("batch", "ctx"), "head"),
        P("head", None),
    )
    out_specs = (P(("batch", "ctx"), "head"), P(("batch", "ctx"), "head"))
    return jax.shard_map(
        functools.partial(per_device, sizes),
        mesh=mesh, in_specs=in_specs, out_specs=out_specs, check_vma=False,
    )
```

```python
import functools
import math

import jax
import jax.numpy as jnp
from jax import lax
from jax.experimental import pallas as pl
from jax.experimental.pallas import tpu as pltpu
from jax.sharding import PartitionSpec as P

HD = 128
RADIUS = 2
AHEAD = 3
MESH = pl.DeviceIdType.MESH


def kernel(
    sizes, queries, keyvals, w_out, out, out_tan,
    q, kv, w, att, acc,
    q_sem, own_sem, w_sem, kv_send, kv_recv, att_send, att_recv,
    wy_send, wy_recv, wb_send, wb_recv,
):
    n_ctx, n_head, n_batch = sizes
    rows = queries.shape[1]
    width = queries.shape[2]
    heads = width // HD
    cols = out.shape[1]
    slots = min(n_ctx, 2 * RADIUS + 1)
    me = lax.axis_index("ctx")
    mine = lax.axis_index("head")
    b = lax.axis_index("batch")
    bits = [2, 1] if n_batch % 4 == 0 else [1] if n_batch % 2 == 0 else []
    pair = 2 if heads % 2 == 0 else 1
    chunk = pair * HD
    chunks = heads // pair
    piece = chunk // (1 << len(bits))

    def slot_of(tile, at):
        return tile if n_ctx <= 2 * RADIUS + 1 else tile - at + RADIUS

    def tile_rows(slot):
        return pl.ds(pl.multiple_of(slot * rows, rows), rows)

    def head_cols(h):
        return pl.ds(h * HD, HD)

    def w_rows(group, first, count):
        return pl.ds(pl.multiple_of(group * width + first, piece), count)

    def w_cols(group):
        return pl.ds(pl.multiple_of(group * cols, 128), cols)

    def sign(d):
        return 1 if d == 0 else -1

    def kv_copy(d, r, h):
        tile = me - sign(d) * (r - 1)
        to = me + sign(d)
        if r == 1:
            src = keyvals.at[:, :, head_cols(h)]
        else:
            src = kv.at[h, :, tile_rows(slot_of(tile, me)), :]
        return pltpu.make_async_remote_copy(
            src_ref=src,
            dst_ref=kv.at[h, :, tile_rows(slot_of(tile, to)), :],
            send_sem=kv_send.at[d, r - 1, h],
            recv_sem=kv_recv.at[d, r - 1, h],
            device_id={"ctx": to},
            device_id_type=MESH,
        )

    def kv_arrival(d, r, h):
        here = kv.at[h, :, tile_rows(slot_of(me - sign(d) * r, me)), :]
        return pltpu.make_async_remote_copy(
            src_ref=here, dst_ref=here,
            send_sem=kv_send.at[d, r - 1, h],
            recv_sem=kv_recv.at[d, r - 1, h],
            device_id={"ctx": me - sign(d)},
            device_id_type=MESH,
        )

    def sends(d, r):
        if d == 0:
            return (me - (r - 1) >= 0) & (me + 1 < n_ctx)
        return (me + (r - 1) < n_ctx) & (me - 1 >= 0)

    def gets(d, r):
        return me - r >= 0 if d == 0 else me + r < n_ctx

    def kv_start(r, h):
        for d in range(2):
            @pl.when(sends(d, r))
            def _():
                kv_copy(d, r, h).start()

    def kv_wait(r, h):
        for d in range(2):
            @pl.when(gets(d, r))
            def _():
                kv_arrival(d, r, h).wait_recv()

    def bit_of(bit):
        return lax.rem(b // bit, 2)

    def partner(bit):
        return b + bit - 2 * bit * bit_of(bit)

    number = 0
    for place, bit in enumerate(bits):
        number = number + bit_of(bit) * (1 << place)

    def wy_copy(d, c):
        peer = lax.rem(mine + d, n_head)
        return pltpu.make_async_remote_copy(
            src_ref=w_out.at[
                pl.ds(pl.multiple_of(c * chunk + number * piece, piece), piece), w_cols(peer)
            ],
            dst_ref=w.at[w_rows(mine, c * chunk + number * piece, piece), :],
            send_sem=wy_send.at[d - 1, c],
            recv_sem=wy_recv.at[d - 1, c],
            device_id={"head": peer},
            device_id_type=MESH,
        )

    def wy_arrival(d, c):
        sender = lax.rem(mine + n_head - d, n_head)
        here = w.at[w_rows(sender, c * chunk + number * piece, piece), :]
        return pltpu.make_async_remote_copy(
            src_ref=here, dst_ref=here,
            send_sem=wy_send.at[d - 1, c], recv_sem=wy_recv.at[d - 1, c],
            device_id={"head": sender}, device_id_type=MESH,
        )

    def wb_copy(level, d, c, receive=False):
        sender = lax.rem(mine + n_head - d, n_head)
        block = piece << level
        index = number // (1 << level)
        if receive:
            index = index + 1 - 2 * lax.rem(index, 2)
        here = w.at[w_rows(sender, c * chunk + index * block, block), :]
        return pltpu.make_async_remote_copy(
            src_ref=here, dst_ref=here,
            send_sem=wb_send.at[level, d - 1, c], recv_sem=wb_recv.at[level, d - 1, c],
            device_id={"batch": partner(bits[level])}, device_id_type=MESH,
        )

    def w_step(stage, c):
        for d in range(1, n_head):
            if stage == 0:
                wy_arrival(d, c).wait_recv()
            else:
                wb_copy(stage - 1, d, c, receive=True).wait_recv()
            if stage < len(bits):
                wb_copy(stage, d, c).start()

    def att_copy(d, h):
        return pltpu.make_async_remote_copy(
            src_ref=att.at[mine, h], dst_ref=att.at[mine, h],
            send_sem=att_send.at[d - 1, h], recv_sem=att_recv.at[d - 1, h],
            device_id={"head": lax.rem(mine + d, n_head)}, device_id_type=MESH,
        )

    def att_arrival(d, h):
        sender = lax.rem(mine + n_head - d, n_head)
        return pltpu.make_async_remote_copy(
            src_ref=att.at[sender, h], dst_ref=att.at[sender, h],
            send_sem=att_send.at[d - 1, h], recv_sem=att_recv.at[d - 1, h],
            device_id={"head": sender}, device_id_type=MESH,
        )

    def q_load():
        return pltpu.make_async_copy(queries, q, q_sem)

    def own_load(h):
        return pltpu.make_async_copy(
            keyvals.at[:, :, head_cols(h)],
            kv.at[h, :, tile_rows(slot_of(me, me)), :],
            own_sem.at[h],
        )

    def w_load():
        return pltpu.make_async_copy(
            w_out.at[:, w_cols(mine)], w.at[w_rows(mine, 0, width), :], w_sem
        )

    barrier = pltpu.get_barrier_semaphore()
    for d in range(2):
        @pl.when(sends(d, 1))
        def _():
            pl.semaphore_signal(
                barrier, inc=1, device_id={"ctx": me + sign(d)}, device_id_type=MESH
            )
    for d in range(1, n_head):
        pl.semaphore_signal(
            barrier, inc=1, device_id={"head": lax.rem(mine + d, n_head)}, device_id_type=MESH
        )
    for bit in bits:
        pl.semaphore_signal(
            barrier, inc=1, device_id={"batch": partner(bit)}, device_id_type=MESH
        )
    q_load().start()
    for h in range(heads):
        own_load(h).start()
    w_load().start()
    base = slot_of(0, me)
    for slot in range(slots):
        tile = slot - base
        @pl.when((tile < 0) | (tile >= n_ctx) | (tile - me > RADIUS) | (me - tile > RADIUS))
        def _():
            kv[:, :, slot * rows:(slot + 1) * rows, :] = jnp.zeros(
                (heads, 4, rows, HD), jnp.bfloat16
            )
    near = jnp.where(me > 0, 1, 0) + jnp.where(me + 1 < n_ctx, 1, 0)
    pl.semaphore_wait(barrier, near + (n_head - 1 + len(bits)))

    for h in range(min(AHEAD, heads)):
        kv_start(1, h)
    for d in range(1, n_head):
        for c in range(chunks):
            wy_copy(d, c).start()

    column_tile = lax.broadcasted_iota(jnp.int32, (1, slots * rows), 1) // rows - base
    visible = (
        (column_tile >= 0) & (column_tile < n_ctx)
        & (column_tile - me <= RADIUS) & (me - column_tile <= RADIUS)
    )
    scale = 1.0 / math.sqrt(HD)

    def attend(h):
        at = slice(h * HD, (h + 1) * HD)
        q_now, q_tan = q[0, :, at], q[1, :, at]
        lhs = jnp.concatenate(
            [
                jnp.concatenate([q_now, jnp.zeros_like(q_now)], axis=1),
                jnp.concatenate([q_tan, q_now], axis=1),
            ],
            axis=0,
        )
        keys = jnp.concatenate([kv[h, 0], kv[h, 2]], axis=1)
        values = jnp.concatenate([kv[h, 1], kv[h, 3]], axis=1)
        both = lax.dot_general(
            lhs, keys, (((1,), (1,)), ((), ())), preferred_element_type=jnp.float32
        )
        scores = jnp.where(visible, both[:rows], -jnp.inf)
        row_max = jnp.max(scores, axis=-1, keepdims=True)
        expo = jnp.exp2((scores - row_max) * (scale * math.log2(math.e)))
        prob = expo * (1.0 / jnp.sum(expo, axis=-1, keepdims=True))
        weighted = prob * (both[rows:] * scale)
        shift = jnp.sum(weighted, axis=-1, keepdims=True)
        left = jnp.concatenate([prob.astype(jnp.bfloat16), weighted.astype(jnp.bfloat16)], axis=0)
        mixed = jnp.dot(left, values, preferred_element_type=jnp.float32)
        attended = mixed[:rows, :HD]
        tangent = mixed[rows:, :HD] + mixed[:rows, HD:] - shift * attended
        att[mine, h, :rows] = attended.astype(jnp.bfloat16)
        att[mine, h, rows:] = tangent.astype(jnp.bfloat16)
        for d in range(1, n_head):
            att_copy(d, h).start()

    def project(group, first, count, fresh=False):
        left = jnp.concatenate([att[group, first + i] for i in range(count)], axis=1)
        part = jnp.dot(
            left, w[w_rows(group, first * HD, count * HD), :], preferred_element_type=jnp.float32
        )
        if fresh:
            acc[...] = part
        else:
            acc[...] += part

    def near_step(h):
        kv_wait(1, h)
        kv_start(2, h)
        if h + AHEAD < heads:
            kv_start(1, h + AHEAD)

    def project_far(c):
        for d in range(1, n_head):
            for i in range(pair):
                att_arrival(d, c * pair + i).wait_recv()
            project(lax.rem(mine + n_head - d, n_head), c * pair, pair)

    arrived = 0
    projected = 0

    def w_steps(step):
        done = 0
        for stage in range(len(bits) + 1):
            if 0 <= step - stage < chunks:
                w_step(stage, step - stage)
                done += stage == len(bits)
        return done

    q_load().wait()
    near_step(0)
    for h in range(heads):
        if h + 1 < heads:
            near_step(h + 1)
        own_load(h).wait()
        kv_wait(2, h)
        attend(h)
        arrived += w_steps(h)
        if h == 0:
            w_load().wait()
        if (h + 1) % pair == 0:
            project(mine, h + 1 - pair, pair, fresh=h + 1 == pair)
        elif projected < arrived and (projected + 1) * pair <= h:
            project_far(projected)
            projected += 1
    for step in range(heads, chunks + len(bits)):
        arrived += w_steps(step)
    for c in range(projected, chunks):
        project_far(c)
    out[...] = acc[:rows].astype(out.dtype)
    out_tan[...] = acc[rows:].astype(out_tan.dtype)

    for h in range(heads):
        for r in range(1, RADIUS + 1):
            for d in range(2):
                @pl.when(sends(d, r))
                def _():
                    kv_copy(d, r, h).wait_send()
        for d in range(1, n_head):
            att_copy(d, h).wait_send()
    for d in range(1, n_head):
        for c in range(chunks):
            wy_copy(d, c).wait_send()
            for level in range(len(bits)):
                wb_copy(level, d, c).wait_send()


def per_device(sizes, queries, keyvals, w_out):
    n_ctx, n_head, n_batch = sizes
    rows, width = queries.shape[1], queries.shape[2]
    heads = width // HD
    cols = w_out.shape[1] // n_head
    slots = min(n_ctx, 2 * RADIUS + 1)
    dma = pltpu.SemaphoreType.DMA
    peers = max(n_head - 1, 1)
    return pl.pallas_call(
        functools.partial(kernel, sizes),
        out_shape=[jax.ShapeDtypeStruct((rows, cols), jnp.bfloat16)] * 2,
        in_specs=[pl.BlockSpec(memory_space=pl.ANY)] * 3,
        out_specs=[pl.BlockSpec(memory_space=pltpu.VMEM)] * 2,
        scratch_shapes=[
            pltpu.VMEM((2, rows, width), jnp.bfloat16),
            pltpu.VMEM((heads, 4, slots * rows, HD), jnp.bfloat16),
            pltpu.VMEM((n_head * width, cols), jnp.bfloat16),
            pltpu.VMEM((n_head, heads, 2 * rows, HD), jnp.bfloat16),
            pltpu.VMEM((2 * rows, cols), jnp.float32),
            dma, dma((heads,)), dma,
            dma((2, RADIUS, heads)), dma((2, RADIUS, heads)),
            dma((peers, heads)), dma((peers, heads)),
            dma((peers, heads)), dma((peers, heads)),
            dma((2, peers, heads)), dma((2, peers, heads)),
        ],
        compiler_params=pltpu.CompilerParams(
            collective_id=0, has_side_effects=True, vmem_limit_bytes=63 * 1024 * 1024
        ),
        cost_estimate=pl.CostEstimate(
            flops=2 * 2 * rows * n_head * width * cols,
            bytes_accessed=16 * rows * width + 2 * w_out.size,
            transcendentals=heads * rows * slots * rows,
        ),
    )(queries, keyvals, w_out)


def solution(mesh):
    sizes = (mesh.shape["ctx"], mesh.shape["head"], mesh.shape["batch"])
    in_specs = (
        P(None, ("batch", "ctx"), "head"),
        P(None, ("batch", "ctx"), "head"),
        P("head", None),
    )
    out_specs = (P(("batch", "ctx"), "head"), P(("batch", "ctx"), "head"))
    return jax.shard_map(
        functools.partial(per_device, sizes),
        mesh=mesh, in_specs=in_specs, out_specs=out_specs, check_vma=False,
    )
```

```python
import functools
import math

import jax
import jax.numpy as jnp
from jax import lax
from jax.experimental import pallas as pl
from jax.experimental.pallas import tpu as pltpu
from jax.sharding import PartitionSpec as P

HD = 128
RADIUS = 2
AHEAD = 3
PIECES = 4
MESH = pl.DeviceIdType.MESH


def kernel(
    sizes, queries, keyvals, w_out, out, out_tan,
    q, kv, w, att, acc,
    q_sem, own_sem, w_sem, kv_send, kv_recv, att_send, att_recv,
    wy_send, wy_recv, wb_send, wb_recv,
):
    n_ctx, n_head, n_batch = sizes
    rows = queries.shape[1]
    width = queries.shape[2]
    heads = width // HD
    cols = out.shape[1]
    slots = min(n_ctx, 2 * RADIUS + 1)
    me = lax.axis_index("ctx")
    mine = lax.axis_index("head")
    b = lax.axis_index("batch")
    bits = [2, 1] if n_batch % 4 == 0 else [1] if n_batch % 2 == 0 else []
    pair = 2 if heads % 2 == 0 else 1
    chunk = pair * HD
    chunks = heads // pair
    piece = chunk // (1 << len(bits))

    def slot_of(tile, at):
        return tile if n_ctx <= 2 * RADIUS + 1 else tile - at + RADIUS

    def tile_rows(slot):
        return pl.ds(pl.multiple_of(slot * rows, rows), rows)

    def head_cols(h):
        return pl.ds(h * HD, HD)

    def w_rows(group, first, count):
        return pl.ds(pl.multiple_of(group * width + first, piece), count)

    def w_cols(group):
        return pl.ds(pl.multiple_of(group * cols, 128), cols)

    def sign(d):
        return 1 if d == 0 else -1

    def kv_copy(d, r, h):
        tile = me - sign(d) * (r - 1)
        to = me + sign(d)
        return pltpu.make_async_remote_copy(
            src_ref=kv.at[h, :, tile_rows(slot_of(tile, me)), :],
            dst_ref=kv.at[h, :, tile_rows(slot_of(tile, to)), :],
            send_sem=kv_send.at[d, r - 1, h],
            recv_sem=kv_recv.at[d, r - 1, h],
            device_id={"ctx": to},
            device_id_type=MESH,
        )

    def kv_arrival(d, r, h):
        here = kv.at[h, :, tile_rows(slot_of(me - sign(d) * r, me)), :]
        return pltpu.make_async_remote_copy(
            src_ref=here, dst_ref=here,
            send_sem=kv_send.at[d, r - 1, h],
            recv_sem=kv_recv.at[d, r - 1, h],
            device_id={"ctx": me - sign(d)},
            device_id_type=MESH,
        )

    def sends(d, r):
        if d == 0:
            return (me - (r - 1) >= 0) & (me + 1 < n_ctx)
        return (me + (r - 1) < n_ctx) & (me - 1 >= 0)

    def gets(d, r):
        return me - r >= 0 if d == 0 else me + r < n_ctx

    def kv_start(r, h):
        for d in range(2):
            @pl.when(sends(d, r))
            def _():
                kv_copy(d, r, h).start()

    def kv_wait(r, h):
        for d in range(2):
            @pl.when(gets(d, r))
            def _():
                kv_arrival(d, r, h).wait_recv()

    def bit_of(bit):
        return lax.rem(b // bit, 2)

    def partner(bit):
        return b + bit - 2 * bit * bit_of(bit)

    number = 0
    for place, bit in enumerate(bits):
        number = number + bit_of(bit) * (1 << place)

    def wy_copy(d, c):
        peer = lax.rem(mine + d, n_head)
        return pltpu.make_async_remote_copy(
            src_ref=w_out.at[
                pl.ds(pl.multiple_of(c * chunk + number * piece, piece), piece), w_cols(peer)
            ],
            dst_ref=w.at[w_rows(mine, c * chunk + number * piece, piece), :],
            send_sem=wy_send.at[d - 1, c],
            recv_sem=wy_recv.at[d - 1, c],
            device_id={"head": peer},
            device_id_type=MESH,
        )

    def wy_arrival(d, c):
        sender = lax.rem(mine + n_head - d, n_head)
        here = w.at[w_rows(sender, c * chunk + number * piece, piece), :]
        return pltpu.make_async_remote_copy(
            src_ref=here, dst_ref=here,
            send_sem=wy_send.at[d - 1, c], recv_sem=wy_recv.at[d - 1, c],
            device_id={"head": sender}, device_id_type=MESH,
        )

    def wb_copy(level, d, c, receive=False):
        sender = lax.rem(mine + n_head - d, n_head)
        block = piece << level
        index = number // (1 << level)
        if receive:
            index = index + 1 - 2 * lax.rem(index, 2)
        here = w.at[w_rows(sender, c * chunk + index * block, block), :]
        return pltpu.make_async_remote_copy(
            src_ref=here, dst_ref=here,
            send_sem=wb_send.at[level, d - 1, c], recv_sem=wb_recv.at[level, d - 1, c],
            device_id={"batch": partner(bits[level])}, device_id_type=MESH,
        )

    def w_step(stage, c):
        for d in range(1, n_head):
            if stage == 0:
                wy_arrival(d, c).wait_recv()
                if c + 1 < chunks:
                    wy_copy(d, c + 1).start()
            else:
                wb_copy(stage - 1, d, c, receive=True).wait_recv()
            if stage < len(bits):
                wb_copy(stage, d, c).start()

    def att_copy(d, h):
        return pltpu.make_async_remote_copy(
            src_ref=att.at[mine, h], dst_ref=att.at[mine, h],
            send_sem=att_send.at[d - 1, h], recv_sem=att_recv.at[d - 1, h],
            device_id={"head": lax.rem(mine + d, n_head)}, device_id_type=MESH,
        )

    def att_arrival(d, h):
        sender = lax.rem(mine + n_head - d, n_head)
        return pltpu.make_async_remote_copy(
            src_ref=att.at[sender, h], dst_ref=att.at[sender, h],
            send_sem=att_send.at[d - 1, h], recv_sem=att_recv.at[d - 1, h],
            device_id={"head": sender}, device_id_type=MESH,
        )

    def q_load():
        return pltpu.make_async_copy(queries, q, q_sem)

    def own_load(h):
        return pltpu.make_async_copy(
            keyvals.at[:, :, head_cols(h)],
            kv.at[h, :, tile_rows(slot_of(me, me)), :],
            own_sem.at[h],
        )

    def w_load():
        return pltpu.make_async_copy(
            w_out.at[:, w_cols(mine)], w.at[w_rows(mine, 0, width), :], w_sem
        )

    barrier = pltpu.get_barrier_semaphore()
    for d in range(2):
        @pl.when(sends(d, 1))
        def _():
            pl.semaphore_signal(
                barrier, inc=1, device_id={"ctx": me + sign(d)}, device_id_type=MESH
            )
    for d in range(1, n_head):
        pl.semaphore_signal(
            barrier, inc=1, device_id={"head": lax.rem(mine + d, n_head)}, device_id_type=MESH
        )
    for bit in bits:
        pl.semaphore_signal(
            barrier, inc=1, device_id={"batch": partner(bit)}, device_id_type=MESH
        )
    q_load().start()
    for h in range(heads):
        own_load(h).start()
    w_load().start()
    base = slot_of(0, me)
    for slot in range(slots):
        tile = slot - base
        @pl.when((tile < 0) | (tile >= n_ctx) | (tile - me > RADIUS) | (me - tile > RADIUS))
        def _():
            kv[:, :, slot * rows:(slot + 1) * rows, :] = jnp.zeros(
                (heads, 4, rows, HD), jnp.bfloat16
            )
    near = jnp.where(me > 0, 1, 0) + jnp.where(me + 1 < n_ctx, 1, 0)
    pl.semaphore_wait(barrier, near + (n_head - 1 + len(bits)))

    for h in range(min(AHEAD, heads)):
        own_load(h).wait()
        kv_start(1, h)
    for d in range(1, n_head):
        wy_copy(d, 0).start()

    column_tile = lax.broadcasted_iota(jnp.int32, (1, slots * rows), 1) // rows - base
    visible = (
        (column_tile >= 0) & (column_tile < n_ctx)
        & (column_tile - me <= RADIUS) & (me - column_tile <= RADIUS)
    )
    scale = 1.0 / math.sqrt(HD)

    def attend(h):
        at = slice(h * HD, (h + 1) * HD)
        q_now, q_tan = q[0, :, at], q[1, :, at]
        lhs = jnp.concatenate(
            [
                jnp.concatenate([q_now, jnp.zeros_like(q_now)], axis=1),
                jnp.concatenate([q_tan, q_now], axis=1),
            ],
            axis=0,
        )
        keys = jnp.concatenate([kv[h, 0], kv[h, 2]], axis=1)
        values = jnp.concatenate([kv[h, 1], kv[h, 3]], axis=1)
        both = lax.dot_general(
            lhs, keys, (((1,), (1,)), ((), ())), preferred_element_type=jnp.float32
        )
        scores = jnp.where(visible, both[:rows], -jnp.inf)
        row_max = jnp.max(scores, axis=-1, keepdims=True)
        expo = jnp.exp2((scores - row_max) * (scale * math.log2(math.e)))
        prob = expo * (1.0 / jnp.sum(expo, axis=-1, keepdims=True))
        weighted = prob * (both[rows:] * scale)
        shift = jnp.sum(weighted, axis=-1, keepdims=True)
        left = jnp.concatenate([prob.astype(jnp.bfloat16), weighted.astype(jnp.bfloat16)], axis=0)
        mixed = jnp.dot(left, values, preferred_element_type=jnp.float32)
        attended = mixed[:rows, :HD]
        tangent = mixed[rows:, :HD] + mixed[:rows, HD:] - shift * attended
        att[mine, h, :rows] = attended.astype(jnp.bfloat16)
        att[mine, h, rows:] = tangent.astype(jnp.bfloat16)
        for d in range(1, n_head):
            att_copy(d, h).start()

    def project(group, first, count, fresh=False):
        left = jnp.concatenate([att[group, first + i] for i in range(count)], axis=1)
        part = jnp.dot(
            left, w[w_rows(group, first * HD, count * HD), :], preferred_element_type=jnp.float32
        )
        if fresh:
            acc[...] = part
        else:
            acc[...] += part

    def near_step(h):
        kv_wait(1, h)
        kv_start(2, h)
        if h + AHEAD < heads:
            own_load(h + AHEAD).wait()
            kv_start(1, h + AHEAD)

    def project_far(c):
        for d in range(1, n_head):
            for i in range(pair):
                att_arrival(d, c * pair + i).wait_recv()
            project(lax.rem(mine + n_head - d, n_head), c * pair, pair)

    arrived = 0
    projected = 0

    def w_steps(step):
        done = 0
        for stage in range(len(bits) + 1):
            if 0 <= step - stage < chunks:
                w_step(stage, step - stage)
                done += stage == len(bits)
        return done

    q_load().wait()
    near_step(0)
    for h in range(heads):
        if h + 1 < heads:
            near_step(h + 1)
        kv_wait(2, h)
        attend(h)
        arrived += w_steps(h)
        if h == 0:
            w_load().wait()
        if (h + 1) % pair == 0:
            project(mine, h + 1 - pair, pair, fresh=h + 1 == pair)
        elif projected < arrived and (projected + 1) * pair <= h:
            project_far(projected)
            projected += 1
    for step in range(heads, chunks + len(bits)):
        arrived += w_steps(step)
    for c in range(projected, chunks):
        project_far(c)
    out[...] = acc[:rows].astype(out.dtype)
    out_tan[...] = acc[rows:].astype(out_tan.dtype)

    for h in range(heads):
        for r in range(1, RADIUS + 1):
            for d in range(2):
                @pl.when(sends(d, r))
                def _():
                    kv_copy(d, r, h).wait_send()
        for d in range(1, n_head):
            att_copy(d, h).wait_send()
    for d in range(1, n_head):
        for c in range(chunks):
            wy_copy(d, c).wait_send()
            for level in range(len(bits)):
                wb_copy(level, d, c).wait_send()


def place(results, results_tan, out, out_tan, sem):
    rows = out.shape[0] // PIECES
    copies = [
        pltpu.make_async_copy(src.at[pl.ds(i * rows, rows)], dst.at[pl.ds(i * rows, rows)], sem.at[n, i])
        for n, (src, dst) in enumerate(((results, out), (results_tan, out_tan)))
        for i in range(PIECES)
    ]
    for copy in copies:
        copy.start()
    for copy in copies:
        copy.wait()


def per_device(sizes, queries, keyvals, w_out):
    n_ctx, n_head, n_batch = sizes
    rows, width = queries.shape[1], queries.shape[2]
    heads = width // HD
    cols = w_out.shape[1] // n_head
    slots = min(n_ctx, 2 * RADIUS + 1)
    dma = pltpu.SemaphoreType.DMA
    peers = max(n_head - 1, 1)
    results = pl.pallas_call(
        functools.partial(kernel, sizes),
        out_shape=[jax.ShapeDtypeStruct((rows, cols), jnp.bfloat16)] * 2,
        in_specs=[pl.BlockSpec(memory_space=pl.ANY)] * 3,
        out_specs=[pl.BlockSpec(memory_space=pltpu.VMEM)] * 2,
        scratch_shapes=[
            pltpu.VMEM((2, rows, width), jnp.bfloat16),
            pltpu.VMEM((heads, 4, slots * rows, HD), jnp.bfloat16),
            pltpu.VMEM((n_head * width, cols), jnp.bfloat16),
            pltpu.VMEM((n_head, heads, 2 * rows, HD), jnp.bfloat16),
            pltpu.VMEM((2 * rows, cols), jnp.float32),
            dma, dma((heads,)), dma,
            dma((2, RADIUS, heads)), dma((2, RADIUS, heads)),
            dma((peers, heads)), dma((peers, heads)),
            dma((peers, heads)), dma((peers, heads)),
            dma((2, peers, heads)), dma((2, peers, heads)),
        ],
        compiler_params=pltpu.CompilerParams(
            collective_id=0, has_side_effects=True, vmem_limit_bytes=63 * 1024 * 1024
        ),
        cost_estimate=pl.CostEstimate(
            flops=2 * 2 * rows * n_head * width * cols,
            bytes_accessed=16 * rows * width + 2 * w_out.size,
            transcendentals=heads * rows * slots * rows,
        ),
    )(queries, keyvals, w_out)
    return pl.pallas_call(
        place,
        out_shape=[jax.ShapeDtypeStruct((rows, cols), jnp.bfloat16)] * 2,
        in_specs=[pl.BlockSpec(memory_space=pl.ANY)] * 2,
        out_specs=[pl.BlockSpec(memory_space=pl.ANY)] * 2,
        scratch_shapes=[dma((2, PIECES))],
    )(*results)


def solution(mesh):
    sizes = (mesh.shape["ctx"], mesh.shape["head"], mesh.shape["batch"])
    in_specs = (
        P(None, ("batch", "ctx"), "head"),
        P(None, ("batch", "ctx"), "head"),
        P("head", None),
    )
    out_specs = (P(("batch", "ctx"), "head"), P(("batch", "ctx"), "head"))
    return jax.shard_map(
        functools.partial(per_device, sizes),
        mesh=mesh, in_specs=in_specs, out_specs=out_specs, check_vma=False,
    )
```

```python
import functools
import math

import jax
import jax.numpy as jnp
from jax import lax
from jax.experimental import pallas as pl
from jax.experimental.pallas import tpu as pltpu
from jax.sharding import PartitionSpec as P

HD = 128
RADIUS = 2
AHEAD = 3
LOOK = 2
PIECES = 4
MESH = pl.DeviceIdType.MESH


def kernel(
    sizes, queries, keyvals, w_out, out, out_tan,
    q, kv, w, att, acc,
    q_sem, own_sem, w_sem, kv_send, kv_recv, att_send, att_recv,
    wy_send, wy_recv, wb_send, wb_recv,
):
    n_ctx, n_head, n_batch = sizes
    rows = queries.shape[1]
    width = queries.shape[2]
    heads = width // HD
    cols = out.shape[1]
    slots = min(n_ctx, 2 * RADIUS + 1)
    me = lax.axis_index("ctx")
    mine = lax.axis_index("head")
    b = lax.axis_index("batch")
    bits = [2, 1] if n_batch % 4 == 0 else [1] if n_batch % 2 == 0 else []
    pair = 2 if heads % 2 == 0 else 1
    chunk = pair * HD
    chunks = heads // pair
    piece = chunk // (1 << len(bits))

    def slot_of(tile, at):
        return tile if n_ctx <= 2 * RADIUS + 1 else tile - at + RADIUS

    def tile_rows(slot):
        return pl.ds(pl.multiple_of(slot * rows, rows), rows)

    def head_cols(h):
        return pl.ds(h * HD, HD)

    def w_rows(group, first, count):
        return pl.ds(pl.multiple_of(group * width + first, piece), count)

    def w_cols(group):
        return pl.ds(pl.multiple_of(group * cols, 128), cols)

    def sign(d):
        return 1 if d == 0 else -1

    def kv_copy(d, r, h):
        tile = me - sign(d) * (r - 1)
        to = me + sign(d)
        return pltpu.make_async_remote_copy(
            src_ref=kv.at[h, :, tile_rows(slot_of(tile, me)), :],
            dst_ref=kv.at[h, :, tile_rows(slot_of(tile, to)), :],
            send_sem=kv_send.at[d, r - 1, h],
            recv_sem=kv_recv.at[d, r - 1, h],
            device_id={"ctx": to},
            device_id_type=MESH,
        )

    def kv_arrival(d, r, h):
        here = kv.at[h, :, tile_rows(slot_of(me - sign(d) * r, me)), :]
        return pltpu.make_async_remote_copy(
            src_ref=here, dst_ref=here,
            send_sem=kv_send.at[d, r - 1, h],
            recv_sem=kv_recv.at[d, r - 1, h],
            device_id={"ctx": me - sign(d)},
            device_id_type=MESH,
        )

    def sends(d, r):
        if d == 0:
            return (me - (r - 1) >= 0) & (me + 1 < n_ctx)
        return (me + (r - 1) < n_ctx) & (me - 1 >= 0)

    def gets(d, r):
        return me - r >= 0 if d == 0 else me + r < n_ctx

    def kv_start(r, h):
        for d in range(2):
            @pl.when(sends(d, r))
            def _():
                kv_copy(d, r, h).start()

    def kv_wait(r, h):
        for d in range(2):
            @pl.when(gets(d, r))
            def _():
                kv_arrival(d, r, h).wait_recv()

    def bit_of(bit):
        return lax.rem(b // bit, 2)

    def partner(bit):
        return b + bit - 2 * bit * bit_of(bit)

    number = 0
    for place, bit in enumerate(bits):
        number = number + bit_of(bit) * (1 << place)

    def wy_copy(d, c):
        peer = lax.rem(mine + d, n_head)
        return pltpu.make_async_remote_copy(
            src_ref=w_out.at[
                pl.ds(pl.multiple_of(c * chunk + number * piece, piece), piece), w_cols(peer)
            ],
            dst_ref=w.at[w_rows(mine, c * chunk + number * piece, piece), :],
            send_sem=wy_send.at[d - 1, c],
            recv_sem=wy_recv.at[d - 1, c],
            device_id={"head": peer},
            device_id_type=MESH,
        )

    def wy_arrival(d, c):
        sender = lax.rem(mine + n_head - d, n_head)
        here = w.at[w_rows(sender, c * chunk + number * piece, piece), :]
        return pltpu.make_async_remote_copy(
            src_ref=here, dst_ref=here,
            send_sem=wy_send.at[d - 1, c], recv_sem=wy_recv.at[d - 1, c],
            device_id={"head": sender}, device_id_type=MESH,
        )

    def wb_copy(level, d, c, receive=False):
        sender = lax.rem(mine + n_head - d, n_head)
        block = piece << level
        index = number // (1 << level)
        if receive:
            index = index + 1 - 2 * lax.rem(index, 2)
        here = w.at[w_rows(sender, c * chunk + index * block, block), :]
        return pltpu.make_async_remote_copy(
            src_ref=here, dst_ref=here,
            send_sem=wb_send.at[level, d - 1, c], recv_sem=wb_recv.at[level, d - 1, c],
            device_id={"batch": partner(bits[level])}, device_id_type=MESH,
        )

    def w_step(stage, c):
        for d in range(1, n_head):
            if stage == 0:
                wy_arrival(d, c).wait_recv()
                if c + 1 < chunks:
                    wy_copy(d, c + 1).start()
            else:
                wb_copy(stage - 1, d, c, receive=True).wait_recv()
            if stage < len(bits):
                wb_copy(stage, d, c).start()

    def att_copy(d, h):
        return pltpu.make_async_remote_copy(
            src_ref=att.at[mine, h], dst_ref=att.at[mine, h],
            send_sem=att_send.at[d - 1, h], recv_sem=att_recv.at[d - 1, h],
            device_id={"head": lax.rem(mine + d, n_head)}, device_id_type=MESH,
        )

    def att_arrival(d, h):
        sender = lax.rem(mine + n_head - d, n_head)
        return pltpu.make_async_remote_copy(
            src_ref=att.at[sender, h], dst_ref=att.at[sender, h],
            send_sem=att_send.at[d - 1, h], recv_sem=att_recv.at[d - 1, h],
            device_id={"head": sender}, device_id_type=MESH,
        )

    def q_load():
        return pltpu.make_async_copy(queries, q, q_sem)

    def own_load(h):
        return pltpu.make_async_copy(
            keyvals.at[:, :, head_cols(h)],
            kv.at[h, :, tile_rows(slot_of(me, me)), :],
            own_sem.at[h],
        )

    def w_load():
        return pltpu.make_async_copy(
            w_out.at[:, w_cols(mine)], w.at[w_rows(mine, 0, width), :], w_sem
        )

    barrier = pltpu.get_barrier_semaphore()
    for d in range(2):
        @pl.when(sends(d, 1))
        def _():
            pl.semaphore_signal(
                barrier, inc=1, device_id={"ctx": me + sign(d)}, device_id_type=MESH
            )
    for d in range(1, n_head):
        pl.semaphore_signal(
            barrier, inc=1, device_id={"head": lax.rem(mine + d, n_head)}, device_id_type=MESH
        )
    for bit in bits:
        pl.semaphore_signal(
            barrier, inc=1, device_id={"batch": partner(bit)}, device_id_type=MESH
        )
    q_load().start()
    for h in range(heads):
        own_load(h).start()
    w_load().start()
    base = slot_of(0, me)
    for slot in range(slots):
        tile = slot - base
        @pl.when((tile < 0) | (tile >= n_ctx) | (tile - me > RADIUS) | (me - tile > RADIUS))
        def _():
            kv[:, :, slot * rows:(slot + 1) * rows, :] = jnp.zeros(
                (heads, 4, rows, HD), jnp.bfloat16
            )
    near = jnp.where(me > 0, 1, 0) + jnp.where(me + 1 < n_ctx, 1, 0)
    pl.semaphore_wait(barrier, near + (n_head - 1 + len(bits)))

    for h in range(min(AHEAD, heads)):
        own_load(h).wait()
        kv_start(1, h)
    for d in range(1, n_head):
        wy_copy(d, 0).start()

    column_tile = lax.broadcasted_iota(jnp.int32, (1, slots * rows), 1) // rows - base
    visible = (
        (column_tile >= 0) & (column_tile < n_ctx)
        & (column_tile - me <= RADIUS) & (me - column_tile <= RADIUS)
    )
    scale = 1.0 / math.sqrt(HD)

    def attend(h):
        at = slice(h * HD, (h + 1) * HD)
        q_now, q_tan = q[0, :, at], q[1, :, at]
        lhs = jnp.concatenate(
            [
                jnp.concatenate([q_now, jnp.zeros_like(q_now)], axis=1),
                jnp.concatenate([q_tan, q_now], axis=1),
            ],
            axis=0,
        )
        keys = jnp.concatenate([kv[h, 0], kv[h, 2]], axis=1)
        values = jnp.concatenate([kv[h, 1], kv[h, 3]], axis=1)
        both = lax.dot_general(
            lhs, keys, (((1,), (1,)), ((), ())), preferred_element_type=jnp.float32
        )
        scores = jnp.where(visible, both[:rows], -jnp.inf)
        row_max = jnp.max(scores, axis=-1, keepdims=True)
        expo = jnp.exp2((scores - row_max) * (scale * math.log2(math.e)))
        prob = expo * (1.0 / jnp.sum(expo, axis=-1, keepdims=True))
        weighted = prob * (both[rows:] * scale)
        shift = jnp.sum(weighted, axis=-1, keepdims=True)
        left = jnp.concatenate([prob.astype(jnp.bfloat16), weighted.astype(jnp.bfloat16)], axis=0)
        mixed = jnp.dot(left, values, preferred_element_type=jnp.float32)
        attended = mixed[:rows, :HD]
        tangent = mixed[rows:, :HD] + mixed[:rows, HD:] - shift * attended
        att[mine, h, :rows] = attended.astype(jnp.bfloat16)
        att[mine, h, rows:] = tangent.astype(jnp.bfloat16)
        for d in range(1, n_head):
            att_copy(d, h).start()

    def project(group, first, count, fresh=False):
        left = jnp.concatenate([att[group, first + i] for i in range(count)], axis=1)
        part = jnp.dot(
            left, w[w_rows(group, first * HD, count * HD), :], preferred_element_type=jnp.float32
        )
        if fresh:
            acc[...] = part
        else:
            acc[...] += part

    def near_step(h):
        kv_wait(1, h)
        kv_start(2, h)
        if h + AHEAD < heads:
            own_load(h + AHEAD).wait()
            kv_start(1, h + AHEAD)

    def project_far(c):
        for d in range(1, n_head):
            for i in range(pair):
                att_arrival(d, c * pair + i).wait_recv()
            project(lax.rem(mine + n_head - d, n_head), c * pair, pair)

    arrived = 0
    projected = 0

    def w_steps(step):
        done = 0
        for stage in range(len(bits) + 1):
            if 0 <= step - stage < chunks:
                w_step(stage, step - stage)
                done += stage == len(bits)
        return done

    q_load().wait()
    for h in range(min(LOOK, heads)):
        near_step(h)
    for h in range(heads):
        if h + LOOK < heads:
            near_step(h + LOOK)
        kv_wait(2, h)
        attend(h)
        arrived += w_steps(h)
        if h == 0:
            w_load().wait()
        if (h + 1) % pair == 0:
            project(mine, h + 1 - pair, pair, fresh=h + 1 == pair)
        elif projected < arrived and (projected + 1) * pair <= h:
            project_far(projected)
            projected += 1
    for step in range(heads, chunks + len(bits)):
        arrived += w_steps(step)
    for c in range(projected, chunks):
        project_far(c)
    out[...] = acc[:rows].astype(out.dtype)
    out_tan[...] = acc[rows:].astype(out_tan.dtype)

    for h in range(heads):
        for r in range(1, RADIUS + 1):
            for d in range(2):
                @pl.when(sends(d, r))
                def _():
                    kv_copy(d, r, h).wait_send()
        for d in range(1, n_head):
            att_copy(d, h).wait_send()
    for d in range(1, n_head):
        for c in range(chunks):
            wy_copy(d, c).wait_send()
            for level in range(len(bits)):
                wb_copy(level, d, c).wait_send()


def place(results, results_tan, out, out_tan, held, in_sem, out_sem):
    rows = out.shape[0] // PIECES
    loads, stores = [], []
    for i in range(PIECES):
        at = pl.ds(i * rows, rows)
        for n, (src, dst) in enumerate(((results, out), (results_tan, out_tan))):
            loads.append(pltpu.make_async_copy(src.at[at], held.at[n, at], in_sem.at[n, i]))
            stores.append(pltpu.make_async_copy(held.at[n, at], dst.at[at], out_sem.at[n, i]))
    for load in loads:
        load.start()
    for load, store in zip(loads, stores):
        load.wait()
        store.start()
    for store in stores:
        store.wait()


def per_device(sizes, queries, keyvals, w_out):
    n_ctx, n_head, n_batch = sizes
    rows, width = queries.shape[1], queries.shape[2]
    heads = width // HD
    cols = w_out.shape[1] // n_head
    slots = min(n_ctx, 2 * RADIUS + 1)
    dma = pltpu.SemaphoreType.DMA
    peers = max(n_head - 1, 1)
    results = pl.pallas_call(
        functools.partial(kernel, sizes),
        out_shape=[jax.ShapeDtypeStruct((rows, cols), jnp.bfloat16)] * 2,
        in_specs=[pl.BlockSpec(memory_space=pl.ANY)] * 3,
        out_specs=[pl.BlockSpec(memory_space=pltpu.VMEM)] * 2,
        scratch_shapes=[
            pltpu.VMEM((2, rows, width), jnp.bfloat16),
            pltpu.VMEM((heads, 4, slots * rows, HD), jnp.bfloat16),
            pltpu.VMEM((n_head * width, cols), jnp.bfloat16),
            pltpu.VMEM((n_head, heads, 2 * rows, HD), jnp.bfloat16),
            pltpu.VMEM((2 * rows, cols), jnp.float32),
            dma, dma((heads,)), dma,
            dma((2, RADIUS, heads)), dma((2, RADIUS, heads)),
            dma((peers, heads)), dma((peers, heads)),
            dma((peers, heads)), dma((peers, heads)),
            dma((2, peers, heads)), dma((2, peers, heads)),
        ],
        compiler_params=pltpu.CompilerParams(
            collective_id=0, has_side_effects=True, vmem_limit_bytes=63 * 1024 * 1024
        ),
        cost_estimate=pl.CostEstimate(
            flops=2 * 2 * rows * n_head * width * cols,
            bytes_accessed=16 * rows * width + 2 * w_out.size,
            transcendentals=heads * rows * slots * rows,
        ),
    )(queries, keyvals, w_out)
    return pl.pallas_call(
        place,
        out_shape=[jax.ShapeDtypeStruct((rows, cols), jnp.bfloat16)] * 2,
        in_specs=[pl.BlockSpec(memory_space=pl.ANY)] * 2,
        out_specs=[pl.BlockSpec(memory_space=pl.ANY)] * 2,
        scratch_shapes=[
            pltpu.VMEM((2, rows, cols), jnp.bfloat16), dma((2, PIECES)), dma((2, PIECES)),
        ],
        compiler_params=pltpu.CompilerParams(vmem_limit_bytes=63 * 1024 * 1024),
    )(*results)


def solution(mesh):
    sizes = (mesh.shape["ctx"], mesh.shape["head"], mesh.shape["batch"])
    in_specs = (
        P(None, ("batch", "ctx"), "head"),
        P(None, ("batch", "ctx"), "head"),
        P("head", None),
    )
    out_specs = (P(("batch", "ctx"), "head"), P(("batch", "ctx"), "head"))
    return jax.shard_map(
        functools.partial(per_device, sizes),
        mesh=mesh, in_specs=in_specs, out_specs=out_specs, check_vma=False,
    )
```

```python
import functools
import math

import jax
import jax.numpy as jnp
from jax import lax
from jax.experimental import pallas as pl
from jax.experimental.pallas import tpu as pltpu
from jax.sharding import PartitionSpec as P

HD = 128
RADIUS = 2
AHEAD = 3
LOOK = 2
PIECES = 4
MESH = pl.DeviceIdType.MESH


def kernel(
    sizes, queries, keyvals, w_out, out, out_tan,
    q, kv, w, att, acc, rounded,
    q_sem, own_sem, out_sem, w_sem, kv_send, kv_recv, att_send, att_recv,
    wy_send, wy_recv, wb_send, wb_recv,
):
    n_ctx, n_head, n_batch = sizes
    rows = queries.shape[1]
    width = queries.shape[2]
    heads = width // HD
    cols = out.shape[1]
    slots = min(n_ctx, 2 * RADIUS + 1)
    me = lax.axis_index("ctx")
    mine = lax.axis_index("head")
    b = lax.axis_index("batch")
    bits = [2, 1] if n_batch % 4 == 0 else [1] if n_batch % 2 == 0 else []
    pair = 2 if heads % 2 == 0 else 1
    chunk = pair * HD
    chunks = heads // pair
    piece = chunk // (1 << len(bits))

    def slot_of(tile, at):
        return tile if n_ctx <= 2 * RADIUS + 1 else tile - at + RADIUS

    def tile_rows(slot):
        return pl.ds(pl.multiple_of(slot * rows, rows), rows)

    def head_cols(h):
        return pl.ds(h * HD, HD)

    def w_rows(group, first, count):
        return pl.ds(pl.multiple_of(group * width + first, piece), count)

    def w_cols(group):
        return pl.ds(pl.multiple_of(group * cols, 128), cols)

    def sign(d):
        return 1 if d == 0 else -1

    def kv_copy(d, r, h, p):
        tile = me - sign(d) * (r - 1)
        to = me + sign(d)
        return pltpu.make_async_remote_copy(
            src_ref=kv.at[h, pl.ds(2 * p, 2), tile_rows(slot_of(tile, me)), :],
            dst_ref=kv.at[h, pl.ds(2 * p, 2), tile_rows(slot_of(tile, to)), :],
            send_sem=kv_send.at[d, r - 1, h, p],
            recv_sem=kv_recv.at[d, r - 1, h, p],
            device_id={"ctx": to},
            device_id_type=MESH,
        )

    def kv_arrival(d, r, h, p):
        here = kv.at[h, pl.ds(2 * p, 2), tile_rows(slot_of(me - sign(d) * r, me)), :]
        return pltpu.make_async_remote_copy(
            src_ref=here, dst_ref=here,
            send_sem=kv_send.at[d, r - 1, h, p],
            recv_sem=kv_recv.at[d, r - 1, h, p],
            device_id={"ctx": me - sign(d)},
            device_id_type=MESH,
        )

    def sends(d, r):
        if d == 0:
            return (me - (r - 1) >= 0) & (me + 1 < n_ctx)
        return (me + (r - 1) < n_ctx) & (me - 1 >= 0)

    def gets(d, r):
        return me - r >= 0 if d == 0 else me + r < n_ctx

    def kv_start(r, h, p):
        for d in range(2):
            @pl.when(sends(d, r))
            def _():
                kv_copy(d, r, h, p).start()

    def kv_wait(r, h, p):
        for d in range(2):
            @pl.when(gets(d, r))
            def _():
                kv_arrival(d, r, h, p).wait_recv()

    def bit_of(bit):
        return lax.rem(b // bit, 2)

    def partner(bit):
        return b + bit - 2 * bit * bit_of(bit)

    number = 0
    for place, bit in enumerate(bits):
        number = number + bit_of(bit) * (1 << place)

    def wy_copy(d, c):
        peer = lax.rem(mine + d, n_head)
        return pltpu.make_async_remote_copy(
            src_ref=w_out.at[
                pl.ds(pl.multiple_of(c * chunk + number * piece, piece), piece), w_cols(peer)
            ],
            dst_ref=w.at[w_rows(mine, c * chunk + number * piece, piece), :],
            send_sem=wy_send.at[d - 1, c],
            recv_sem=wy_recv.at[d - 1, c],
            device_id={"head": peer},
            device_id_type=MESH,
        )

    def wy_arrival(d, c):
        sender = lax.rem(mine + n_head - d, n_head)
        here = w.at[w_rows(sender, c * chunk + number * piece, piece), :]
        return pltpu.make_async_remote_copy(
            src_ref=here, dst_ref=here,
            send_sem=wy_send.at[d - 1, c], recv_sem=wy_recv.at[d - 1, c],
            device_id={"head": sender}, device_id_type=MESH,
        )

    def wb_copy(level, d, c, receive=False):
        sender = lax.rem(mine + n_head - d, n_head)
        block = piece << level
        index = number // (1 << level)
        if receive:
            index = index + 1 - 2 * lax.rem(index, 2)
        here = w.at[w_rows(sender, c * chunk + index * block, block), :]
        return pltpu.make_async_remote_copy(
            src_ref=here, dst_ref=here,
            send_sem=wb_send.at[level, d - 1, c], recv_sem=wb_recv.at[level, d - 1, c],
            device_id={"batch": partner(bits[level])}, device_id_type=MESH,
        )

    def w_step(stage, c):
        for d in range(1, n_head):
            if stage == 0:
                wy_arrival(d, c).wait_recv()
                if c + 1 < chunks:
                    wy_copy(d, c + 1).start()
            else:
                wb_copy(stage - 1, d, c, receive=True).wait_recv()
            if stage < len(bits):
                wb_copy(stage, d, c).start()

    def att_copy(d, h):
        return pltpu.make_async_remote_copy(
            src_ref=att.at[mine, h], dst_ref=att.at[mine, h],
            send_sem=att_send.at[d - 1, h], recv_sem=att_recv.at[d - 1, h],
            device_id={"head": lax.rem(mine + d, n_head)}, device_id_type=MESH,
        )

    def att_arrival(d, h):
        sender = lax.rem(mine + n_head - d, n_head)
        return pltpu.make_async_remote_copy(
            src_ref=att.at[sender, h], dst_ref=att.at[sender, h],
            send_sem=att_send.at[d - 1, h], recv_sem=att_recv.at[d - 1, h],
            device_id={"head": sender}, device_id_type=MESH,
        )

    def q_load():
        return pltpu.make_async_copy(queries, q, q_sem)

    def own_load(h, p):
        return [
            pltpu.make_async_copy(
                keyvals.at[2 * i + p, :, head_cols(h)],
                kv.at[h, 2 * p + i, tile_rows(slot_of(me, me)), :],
                own_sem.at[h, 2 * p + i],
            )
            for i in range(2)
        ]

    def own_send(h):
        for p in range(2):
            for load in own_load(h, p):
                load.wait()
            kv_start(1, h, p)

    def w_load():
        return pltpu.make_async_copy(
            w_out.at[:, w_cols(mine)], w.at[w_rows(mine, 0, width), :], w_sem
        )

    barrier = pltpu.get_barrier_semaphore()
    for d in range(2):
        @pl.when(sends(d, 1))
        def _():
            pl.semaphore_signal(
                barrier, inc=1, device_id={"ctx": me + sign(d)}, device_id_type=MESH
            )
    for d in range(1, n_head):
        pl.semaphore_signal(
            barrier, inc=1, device_id={"head": lax.rem(mine + d, n_head)}, device_id_type=MESH
        )
    for bit in bits:
        pl.semaphore_signal(
            barrier, inc=1, device_id={"batch": partner(bit)}, device_id_type=MESH
        )
    q_load().start()
    for h in range(heads):
        for p in range(2):
            for load in own_load(h, p):
                load.start()
    w_load().start()
    base = slot_of(0, me)
    for slot in range(slots):
        tile = slot - base
        @pl.when((tile < 0) | (tile >= n_ctx) | (tile - me > RADIUS) | (me - tile > RADIUS))
        def _():
            kv[:, :, slot * rows:(slot + 1) * rows, :] = jnp.zeros(
                (heads, 4, rows, HD), jnp.bfloat16
            )
    near = jnp.where(me > 0, 1, 0) + jnp.where(me + 1 < n_ctx, 1, 0)
    pl.semaphore_wait(barrier, near + (n_head - 1 + len(bits)))

    for h in range(min(AHEAD, heads)):
        own_send(h)
    for d in range(1, n_head):
        wy_copy(d, 0).start()

    column_tile = lax.broadcasted_iota(jnp.int32, (1, slots * rows), 1) // rows - base
    visible = (
        (column_tile >= 0) & (column_tile < n_ctx)
        & (column_tile - me <= RADIUS) & (me - column_tile <= RADIUS)
    )
    scale = 1.0 / math.sqrt(HD)

    def attend(h):
        at = slice(h * HD, (h + 1) * HD)
        q_now, q_tan = q[0, :, at], q[1, :, at]
        lhs = jnp.concatenate(
            [
                jnp.concatenate([q_now, jnp.zeros_like(q_now)], axis=1),
                jnp.concatenate([q_tan, q_now], axis=1),
            ],
            axis=0,
        )
        kv_wait(2, h, 0)
        keys = jnp.concatenate([kv[h, 0], kv[h, 1]], axis=1)
        both = lax.dot_general(
            lhs, keys, (((1,), (1,)), ((), ())), preferred_element_type=jnp.float32
        )
        scores = jnp.where(visible, both[:rows], -jnp.inf)
        row_max = jnp.max(scores, axis=-1, keepdims=True)
        expo = jnp.exp2((scores - row_max) * (scale * math.log2(math.e)))
        prob = expo * (1.0 / jnp.sum(expo, axis=-1, keepdims=True))
        weighted = prob * (both[rows:] * scale)
        shift = jnp.sum(weighted, axis=-1, keepdims=True)
        left = jnp.concatenate([prob.astype(jnp.bfloat16), weighted.astype(jnp.bfloat16)], axis=0)
        kv_wait(2, h, 1)
        values = jnp.concatenate([kv[h, 2], kv[h, 3]], axis=1)
        mixed = jnp.dot(left, values, preferred_element_type=jnp.float32)
        attended = mixed[:rows, :HD]
        tangent = mixed[rows:, :HD] + mixed[:rows, HD:] - shift * attended
        att[mine, h, :rows] = attended.astype(jnp.bfloat16)
        att[mine, h, rows:] = tangent.astype(jnp.bfloat16)
        for d in range(1, n_head):
            att_copy(d, h).start()

    block = 512 if cols % 512 == 0 else cols

    def out_copies(i):
        at = pl.ds(i * block, block)
        return [
            pltpu.make_async_copy(rounded.at[pl.ds(n * rows, rows), at], to.at[:, at], out_sem.at[n, i])
            for n, to in enumerate((out, out_tan))
        ]

    def finish(group, first, count):
        left = jnp.concatenate([att[group, first + i] for i in range(count)], axis=1)
        for i in range(cols // block):
            at = slice(i * block, (i + 1) * block)
            part = jnp.dot(
                left, w[w_rows(group, first * HD, count * HD), at],
                preferred_element_type=jnp.float32,
            )
            rounded[:, at] = (acc[:, at] + part).astype(rounded.dtype)
            for copy in out_copies(i):
                copy.start()

    def project(group, first, count, fresh=False):
        left = jnp.concatenate([att[group, first + i] for i in range(count)], axis=1)
        part = jnp.dot(
            left, w[w_rows(group, first * HD, count * HD), :], preferred_element_type=jnp.float32
        )
        if fresh:
            acc[...] = part
        else:
            acc[...] += part

    def near_step(h):
        for p in range(2):
            kv_wait(1, h, p)
            kv_start(2, h, p)
        if h + AHEAD < heads:
            own_send(h + AHEAD)

    def project_far(c):
        for d in range(1, n_head):
            for i in range(pair):
                att_arrival(d, c * pair + i).wait_recv()
            last = c == chunks - 1 and d == n_head - 1
            (finish if last else project)(lax.rem(mine + n_head - d, n_head), c * pair, pair)

    arrived = 0
    projected = 0

    def w_steps(step):
        done = 0
        for stage in range(len(bits) + 1):
            if 0 <= step - stage < chunks:
                w_step(stage, step - stage)
                done += stage == len(bits)
        return done

    q_load().wait()
    for h in range(min(LOOK, heads)):
        near_step(h)
    for h in range(heads):
        if h + LOOK < heads:
            near_step(h + LOOK)
        attend(h)
        arrived += w_steps(h)
        if h == 0:
            w_load().wait()
        if (h + 1) % pair == 0:
            project(mine, h + 1 - pair, pair, fresh=h + 1 == pair)
        elif projected < arrived and (projected + 1) * pair <= h:
            project_far(projected)
            projected += 1
    for step in range(heads, chunks + len(bits)):
        arrived += w_steps(step)
    for c in range(projected, chunks):
        project_far(c)
    for h in range(heads):
        for r in range(1, RADIUS + 1):
            for d in range(2):
                @pl.when(sends(d, r))
                def _():
                    kv_copy(d, r, h, 0).wait_send()
                    kv_copy(d, r, h, 1).wait_send()
        for d in range(1, n_head):
            att_copy(d, h).wait_send()
    for d in range(1, n_head):
        for c in range(chunks):
            wy_copy(d, c).wait_send()
            for level in range(len(bits)):
                wb_copy(level, d, c).wait_send()
    for i in range(cols // block):
        for copy in out_copies(i):
            copy.wait()


def place(results, results_tan, out, out_tan, held, in_sem, out_sem):
    rows = out.shape[0] // PIECES
    loads, stores = [], []
    for i in range(PIECES):
        at = pl.ds(i * rows, rows)
        for n, (src, dst) in enumerate(((results, out), (results_tan, out_tan))):
            loads.append(pltpu.make_async_copy(src.at[at], held.at[n, at], in_sem.at[n, i]))
            stores.append(pltpu.make_async_copy(held.at[n, at], dst.at[at], out_sem.at[n, i]))
    for load in loads:
        load.start()
    for load, store in zip(loads, stores):
        load.wait()
        store.start()
    for store in stores:
        store.wait()


def per_device(sizes, queries, keyvals, w_out):
    n_ctx, n_head, n_batch = sizes
    rows, width = queries.shape[1], queries.shape[2]
    heads = width // HD
    cols = w_out.shape[1] // n_head
    slots = min(n_ctx, 2 * RADIUS + 1)
    dma = pltpu.SemaphoreType.DMA
    peers = max(n_head - 1, 1)
    results = pl.pallas_call(
        functools.partial(kernel, sizes),
        out_shape=[jax.ShapeDtypeStruct((rows, cols), jnp.bfloat16)] * 2,
        in_specs=[pl.BlockSpec(memory_space=pl.ANY)] * 3,
        out_specs=[pl.BlockSpec(memory_space=pl.ANY)] * 2,
        scratch_shapes=[
            pltpu.VMEM((2, rows, width), jnp.bfloat16),
            pltpu.VMEM((heads, 4, slots * rows, HD), jnp.bfloat16),
            pltpu.VMEM((n_head * width, cols), jnp.bfloat16),
            pltpu.VMEM((n_head, heads, 2 * rows, HD), jnp.bfloat16),
            pltpu.VMEM((2 * rows, cols), jnp.float32),
            pltpu.VMEM((2 * rows, cols), jnp.bfloat16),
            dma, dma((heads, 4)), dma((2, cols // HD)), dma,
            dma((2, RADIUS, heads, 2)), dma((2, RADIUS, heads, 2)),
            dma((peers, heads)), dma((peers, heads)),
            dma((peers, heads)), dma((peers, heads)),
            dma((2, peers, heads)), dma((2, peers, heads)),
        ],
        compiler_params=pltpu.CompilerParams(
            collective_id=0, has_side_effects=True, vmem_limit_bytes=63 * 1024 * 1024
        ),
        cost_estimate=pl.CostEstimate(
            flops=2 * 2 * rows * n_head * width * cols,
            bytes_accessed=16 * rows * width + 2 * w_out.size,
            transcendentals=heads * rows * slots * rows,
        ),
    )(queries, keyvals, w_out)
    return pl.pallas_call(
        place,
        out_shape=[jax.ShapeDtypeStruct((rows, cols), jnp.bfloat16)] * 2,
        in_specs=[pl.BlockSpec(memory_space=pl.ANY)] * 2,
        out_specs=[pl.BlockSpec(memory_space=pl.ANY)] * 2,
        scratch_shapes=[
            pltpu.VMEM((2, rows, cols), jnp.bfloat16), dma((2, PIECES)), dma((2, PIECES)),
        ],
        compiler_params=pltpu.CompilerParams(vmem_limit_bytes=63 * 1024 * 1024),
    )(*results)


def solution(mesh):
    sizes = (mesh.shape["ctx"], mesh.shape["head"], mesh.shape["batch"])
    in_specs = (
        P(None, ("batch", "ctx"), "head"),
        P(None, ("batch", "ctx"), "head"),
        P("head", None),
    )
    out_specs = (P(("batch", "ctx"), "head"), P(("batch", "ctx"), "head"))
    return jax.shard_map(
        functools.partial(per_device, sizes),
        mesh=mesh, in_specs=in_specs, out_specs=out_specs, check_vma=False,
    )
```

```python
import functools
import math

import jax
import jax.numpy as jnp
from jax import lax
from jax.experimental import pallas as pl
from jax.experimental.pallas import tpu as pltpu
from jax.sharding import PartitionSpec as P

HD = 128
RADIUS = 2
AHEAD = 6
LOOK = 4
PIECES = 4
MESH = pl.DeviceIdType.MESH


def kernel(
    sizes, queries, keyvals, w_out, out, out_tan,
    q, kv, w, att, acc, rounded,
    q_sem, own_sem, out_sem, w_sem, kv_send, kv_recv, att_send, att_recv,
    wy_send, wy_recv, wb_send, wb_recv,
):
    n_ctx, n_head, n_batch = sizes
    rows = queries.shape[1]
    width = queries.shape[2]
    heads = width // HD
    cols = out.shape[1]
    slots = min(n_ctx, 2 * RADIUS + 1)
    me = lax.axis_index("ctx")
    mine = lax.axis_index("head")
    b = lax.axis_index("batch")
    bits = [2, 1] if n_batch % 4 == 0 else [1] if n_batch % 2 == 0 else []
    pair = 2 if heads % 2 == 0 else 1
    chunk = pair * HD
    chunks = heads // pair
    piece = chunk // (1 << len(bits))

    def slot_of(tile, at):
        return tile if n_ctx <= 2 * RADIUS + 1 else tile - at + RADIUS

    def tile_rows(slot):
        return pl.ds(pl.multiple_of(slot * rows, rows), rows)

    def head_cols(h):
        return pl.ds(h * HD, HD)

    def w_rows(group, first, count):
        return pl.ds(pl.multiple_of(group * width + first, piece), count)

    def w_cols(group):
        return pl.ds(pl.multiple_of(group * cols, 128), cols)

    def sign(d):
        return 1 if d == 0 else -1

    def kv_copy(d, r, h, p):
        tile = me - sign(d) * (r - 1)
        to = me + sign(d)
        return pltpu.make_async_remote_copy(
            src_ref=kv.at[h, pl.ds(2 * p, 2), tile_rows(slot_of(tile, me)), :],
            dst_ref=kv.at[h, pl.ds(2 * p, 2), tile_rows(slot_of(tile, to)), :],
            send_sem=kv_send.at[d, r - 1, h, p],
            recv_sem=kv_recv.at[d, r - 1, h, p],
            device_id={"ctx": to},
            device_id_type=MESH,
        )

    def kv_arrival(d, r, h, p):
        here = kv.at[h, pl.ds(2 * p, 2), tile_rows(slot_of(me - sign(d) * r, me)), :]
        return pltpu.make_async_remote_copy(
            src_ref=here, dst_ref=here,
            send_sem=kv_send.at[d, r - 1, h, p],
            recv_sem=kv_recv.at[d, r - 1, h, p],
            device_id={"ctx": me - sign(d)},
            device_id_type=MESH,
        )

    def sends(d, r):
        if d == 0:
            return (me - (r - 1) >= 0) & (me + 1 < n_ctx)
        return (me + (r - 1) < n_ctx) & (me - 1 >= 0)

    def gets(d, r):
        return me - r >= 0 if d == 0 else me + r < n_ctx

    def kv_start(r, h, p):
        for d in range(2):
            @pl.when(sends(d, r))
            def _():
                kv_copy(d, r, h, p).start()

    def kv_wait(r, h, p):
        for d in range(2):
            @pl.when(gets(d, r))
            def _():
                kv_arrival(d, r, h, p).wait_recv()

    def bit_of(bit):
        return lax.rem(b // bit, 2)

    def partner(bit):
        return b + bit - 2 * bit * bit_of(bit)

    number = 0
    for place, bit in enumerate(bits):
        number = number + bit_of(bit) * (1 << place)

    def wy_copy(d, c):
        peer = lax.rem(mine + d, n_head)
        return pltpu.make_async_remote_copy(
            src_ref=w_out.at[
                pl.ds(pl.multiple_of(c * chunk + number * piece, piece), piece), w_cols(peer)
            ],
            dst_ref=w.at[w_rows(mine, c * chunk + number * piece, piece), :],
            send_sem=wy_send.at[d - 1, c],
            recv_sem=wy_recv.at[d - 1, c],
            device_id={"head": peer},
            device_id_type=MESH,
        )

    def wy_arrival(d, c):
        sender = lax.rem(mine + n_head - d, n_head)
        here = w.at[w_rows(sender, c * chunk + number * piece, piece), :]
        return pltpu.make_async_remote_copy(
            src_ref=here, dst_ref=here,
            send_sem=wy_send.at[d - 1, c], recv_sem=wy_recv.at[d - 1, c],
            device_id={"head": sender}, device_id_type=MESH,
        )

    def wb_copy(level, d, c, receive=False):
        sender = lax.rem(mine + n_head - d, n_head)
        block = piece << level
        index = number // (1 << level)
        if receive:
            index = index + 1 - 2 * lax.rem(index, 2)
        here = w.at[w_rows(sender, c * chunk + index * block, block), :]
        return pltpu.make_async_remote_copy(
            src_ref=here, dst_ref=here,
            send_sem=wb_send.at[level, d - 1, c], recv_sem=wb_recv.at[level, d - 1, c],
            device_id={"batch": partner(bits[level])}, device_id_type=MESH,
        )

    def w_step(stage, c):
        for d in range(1, n_head):
            if stage == 0:
                wy_arrival(d, c).wait_recv()
                if c + 1 < chunks:
                    wy_copy(d, c + 1).start()
            else:
                wb_copy(stage - 1, d, c, receive=True).wait_recv()
            if stage < len(bits):
                wb_copy(stage, d, c).start()

    def att_copy(d, h):
        return pltpu.make_async_remote_copy(
            src_ref=att.at[mine, h], dst_ref=att.at[mine, h],
            send_sem=att_send.at[d - 1, h], recv_sem=att_recv.at[d - 1, h],
            device_id={"head": lax.rem(mine + d, n_head)}, device_id_type=MESH,
        )

    def att_arrival(d, h):
        sender = lax.rem(mine + n_head - d, n_head)
        return pltpu.make_async_remote_copy(
            src_ref=att.at[sender, h], dst_ref=att.at[sender, h],
            send_sem=att_send.at[d - 1, h], recv_sem=att_recv.at[d - 1, h],
            device_id={"head": sender}, device_id_type=MESH,
        )

    def q_load():
        return pltpu.make_async_copy(queries, q, q_sem)

    def own_load(h, p):
        return [
            pltpu.make_async_copy(
                keyvals.at[2 * i + p, :, head_cols(h)],
                kv.at[h, 2 * p + i, tile_rows(slot_of(me, me)), :],
                own_sem.at[h, 2 * p + i],
            )
            for i in range(2)
        ]

    def own_send(h):
        for p in range(2):
            for load in own_load(h, p):
                load.wait()
            kv_start(1, h, p)

    def w_load():
        return pltpu.make_async_copy(
            w_out.at[:, w_cols(mine)], w.at[w_rows(mine, 0, width), :], w_sem
        )

    barrier = pltpu.get_barrier_semaphore()
    for d in range(2):
        @pl.when(sends(d, 1))
        def _():
            pl.semaphore_signal(
                barrier, inc=1, device_id={"ctx": me + sign(d)}, device_id_type=MESH
            )
    for d in range(1, n_head):
        pl.semaphore_signal(
            barrier, inc=1, device_id={"head": lax.rem(mine + d, n_head)}, device_id_type=MESH
        )
    for bit in bits:
        pl.semaphore_signal(
            barrier, inc=1, device_id={"batch": partner(bit)}, device_id_type=MESH
        )
    q_load().start()
    for h in range(heads):
        for p in range(2):
            for load in own_load(h, p):
                load.start()
    w_load().start()
    base = slot_of(0, me)
    for slot in range(slots):
        tile = slot - base
        @pl.when((tile < 0) | (tile >= n_ctx) | (tile - me > RADIUS) | (me - tile > RADIUS))
        def _():
            kv[:, :, slot * rows:(slot + 1) * rows, :] = jnp.zeros(
                (heads, 4, rows, HD), jnp.bfloat16
            )
    near = jnp.where(me > 0, 1, 0) + jnp.where(me + 1 < n_ctx, 1, 0)
    pl.semaphore_wait(barrier, near + (n_head - 1 + len(bits)))

    for h in range(min(AHEAD, heads)):
        own_send(h)
    for d in range(1, n_head):
        wy_copy(d, 0).start()

    column_tile = lax.broadcasted_iota(jnp.int32, (1, slots * rows), 1) // rows - base
    visible = (
        (column_tile >= 0) & (column_tile < n_ctx)
        & (column_tile - me <= RADIUS) & (me - column_tile <= RADIUS)
    )
    scale = 1.0 / math.sqrt(HD)

    def attend(h):
        at = slice(h * HD, (h + 1) * HD)
        q_now, q_tan = q[0, :, at], q[1, :, at]
        lhs = jnp.concatenate(
            [
                jnp.concatenate([q_now, jnp.zeros_like(q_now)], axis=1),
                jnp.concatenate([q_tan, q_now], axis=1),
            ],
            axis=0,
        )
        kv_wait(2, h, 0)
        keys = jnp.concatenate([kv[h, 0], kv[h, 1]], axis=1)
        both = lax.dot_general(
            lhs, keys, (((1,), (1,)), ((), ())), preferred_element_type=jnp.float32
        )
        scores = jnp.where(visible, both[:rows], -jnp.inf)
        row_max = jnp.max(scores, axis=-1, keepdims=True)
        expo = jnp.exp2((scores - row_max) * (scale * math.log2(math.e)))
        prob = expo * (1.0 / jnp.sum(expo, axis=-1, keepdims=True))
        weighted = prob * (both[rows:] * scale)
        shift = jnp.sum(weighted, axis=-1, keepdims=True)
        left = jnp.concatenate([prob.astype(jnp.bfloat16), weighted.astype(jnp.bfloat16)], axis=0)
        kv_wait(2, h, 1)
        values = jnp.concatenate([kv[h, 2], kv[h, 3]], axis=1)
        mixed = jnp.dot(left, values, preferred_element_type=jnp.float32)
        attended = mixed[:rows, :HD]
        tangent = mixed[rows:, :HD] + mixed[:rows, HD:] - shift * attended
        att[mine, h, :rows] = attended.astype(jnp.bfloat16)
        att[mine, h, rows:] = tangent.astype(jnp.bfloat16)
        for d in range(1, n_head):
            att_copy(d, h).start()

    block = 512 if cols % 512 == 0 else cols

    def out_copies(i):
        at = pl.ds(i * block, block)
        return [
            pltpu.make_async_copy(rounded.at[pl.ds(n * rows, rows), at], to.at[:, at], out_sem.at[n, i])
            for n, to in enumerate((out, out_tan))
        ]

    def finish(group, first, count):
        left = jnp.concatenate([att[group, first + i] for i in range(count)], axis=1)
        for i in range(cols // block):
            at = slice(i * block, (i + 1) * block)
            part = jnp.dot(
                left, w[w_rows(group, first * HD, count * HD), at],
                preferred_element_type=jnp.float32,
            )
            rounded[:, at] = (acc[:, at] + part).astype(rounded.dtype)
            for copy in out_copies(i):
                copy.start()

    def project(group, first, count, fresh=False):
        left = jnp.concatenate([att[group, first + i] for i in range(count)], axis=1)
        part = jnp.dot(
            left, w[w_rows(group, first * HD, count * HD), :], preferred_element_type=jnp.float32
        )
        if fresh:
            acc[...] = part
        else:
            acc[...] += part

    def near_step(h):
        for p in range(2):
            kv_wait(1, h, p)
            kv_start(2, h, p)
        if h + AHEAD < heads:
            own_send(h + AHEAD)

    def project_far(c):
        for d in range(1, n_head):
            for i in range(pair):
                att_arrival(d, c * pair + i).wait_recv()
            last = c == chunks - 1 and d == n_head - 1
            (finish if last else project)(lax.rem(mine + n_head - d, n_head), c * pair, pair)

    arrived = 0
    projected = 0

    def w_steps(step):
        done = 0
        for stage in range(len(bits) + 1):
            if 0 <= step - stage < chunks:
                w_step(stage, step - stage)
                done += stage == len(bits)
        return done

    q_load().wait()
    for h in range(min(LOOK, heads)):
        near_step(h)
    for h in range(heads):
        if h + LOOK < heads:
            near_step(h + LOOK)
        attend(h)
        arrived += w_steps(h)
        if h == 0:
            w_load().wait()
        if (h + 1) % pair == 0:
            project(mine, h + 1 - pair, pair, fresh=h + 1 == pair)
        elif projected < arrived and (projected + 1) * pair <= h:
            project_far(projected)
            projected += 1
    for step in range(heads, chunks + len(bits)):
        arrived += w_steps(step)
    for c in range(projected, chunks):
        project_far(c)
    for h in range(heads):
        for r in range(1, RADIUS + 1):
            for d in range(2):
                @pl.when(sends(d, r))
                def _():
                    kv_copy(d, r, h, 0).wait_send()
                    kv_copy(d, r, h, 1).wait_send()
        for d in range(1, n_head):
            att_copy(d, h).wait_send()
    for d in range(1, n_head):
        for c in range(chunks):
            wy_copy(d, c).wait_send()
            for level in range(len(bits)):
                wb_copy(level, d, c).wait_send()
    for i in range(cols // block):
        for copy in out_copies(i):
            copy.wait()


def place(results, results_tan, out, out_tan, held, in_sem, out_sem):
    rows = out.shape[0] // PIECES
    loads, stores = [], []
    for i in range(PIECES):
        at = pl.ds(i * rows, rows)
        for n, (src, dst) in enumerate(((results, out), (results_tan, out_tan))):
            loads.append(pltpu.make_async_copy(src.at[at], held.at[n, at], in_sem.at[n, i]))
            stores.append(pltpu.make_async_copy(held.at[n, at], dst.at[at], out_sem.at[n, i]))
    for load in loads:
        load.start()
    for load, store in zip(loads, stores):
        load.wait()
        store.start()
    for store in stores:
        store.wait()


def per_device(sizes, queries, keyvals, w_out):
    n_ctx, n_head, n_batch = sizes
    rows, width = queries.shape[1], queries.shape[2]
    heads = width // HD
    cols = w_out.shape[1] // n_head
    slots = min(n_ctx, 2 * RADIUS + 1)
    dma = pltpu.SemaphoreType.DMA
    peers = max(n_head - 1, 1)
    results = pl.pallas_call(
        functools.partial(kernel, sizes),
        out_shape=[jax.ShapeDtypeStruct((rows, cols), jnp.bfloat16)] * 2,
        in_specs=[pl.BlockSpec(memory_space=pl.ANY)] * 3,
        out_specs=[pl.BlockSpec(memory_space=pl.ANY)] * 2,
        scratch_shapes=[
            pltpu.VMEM((2, rows, width), jnp.bfloat16),
            pltpu.VMEM((heads, 4, slots * rows, HD), jnp.bfloat16),
            pltpu.VMEM((n_head * width, cols), jnp.bfloat16),
            pltpu.VMEM((n_head, heads, 2 * rows, HD), jnp.bfloat16),
            pltpu.VMEM((2 * rows, cols), jnp.float32),
            pltpu.VMEM((2 * rows, cols), jnp.bfloat16),
            dma, dma((heads, 4)), dma((2, cols // HD)), dma,
            dma((2, RADIUS, heads, 2)), dma((2, RADIUS, heads, 2)),
            dma((peers, heads)), dma((peers, heads)),
            dma((peers, heads)), dma((peers, heads)),
            dma((2, peers, heads)), dma((2, peers, heads)),
        ],
        compiler_params=pltpu.CompilerParams(
            collective_id=0, has_side_effects=True, vmem_limit_bytes=63 * 1024 * 1024
        ),
        cost_estimate=pl.CostEstimate(
            flops=2 * 2 * rows * n_head * width * cols,
            bytes_accessed=16 * rows * width + 2 * w_out.size,
            transcendentals=heads * rows * slots * rows,
        ),
    )(queries, keyvals, w_out)
    return pl.pallas_call(
        place,
        out_shape=[jax.ShapeDtypeStruct((rows, cols), jnp.bfloat16)] * 2,
        in_specs=[pl.BlockSpec(memory_space=pl.ANY)] * 2,
        out_specs=[pl.BlockSpec(memory_space=pl.ANY)] * 2,
        scratch_shapes=[
            pltpu.VMEM((2, rows, cols), jnp.bfloat16), dma((2, PIECES)), dma((2, PIECES)),
        ],
        compiler_params=pltpu.CompilerParams(vmem_limit_bytes=63 * 1024 * 1024),
    )(*results)


def solution(mesh):
    sizes = (mesh.shape["ctx"], mesh.shape["head"], mesh.shape["batch"])
    in_specs = (
        P(None, ("batch", "ctx"), "head"),
        P(None, ("batch", "ctx"), "head"),
        P("head", None),
    )
    out_specs = (P(("batch", "ctx"), "head"), P(("batch", "ctx"), "head"))
    return jax.shard_map(
        functools.partial(per_device, sizes),
        mesh=mesh, in_specs=in_specs, out_specs=out_specs, check_vma=False,
    )
```

```python
import functools
import math

import jax
import jax.numpy as jnp
from jax import lax
from jax.experimental import pallas as pl
from jax.experimental.pallas import tpu as pltpu
from jax.sharding import PartitionSpec as P

HD = 128
RADIUS = 2
AHEAD = 2
PIECES = 4
MESH = pl.DeviceIdType.MESH


def kernel(
    sizes, queries, keyvals, w_out, out, out_tan,
    q, kv, w, att, acc, rounded, state,
    q_sem, own_sem, out_sem, w_sem, kv_send, kv_recv, att_send, att_recv,
    wy_send, wy_recv, wb_send, wb_recv,
):
    n_ctx, n_head, n_batch = sizes
    rows = queries.shape[1]
    width = queries.shape[2]
    heads = width // HD
    cols = out.shape[1]
    me = lax.axis_index("ctx")
    mine = lax.axis_index("head")
    b = lax.axis_index("batch")
    bits = [2, 1] if n_batch % 4 == 0 else [1] if n_batch % 2 == 0 else []
    pair = 2 if heads % 2 == 0 else 1
    chunk = pair * HD
    chunks = heads // pair
    piece = chunk // (1 << len(bits))

    def tile_rows(d, r):
        slot = 0 if r == 0 else 2 * r - 1 + d
        return pl.ds(slot * rows, rows)

    def head_cols(h):
        return pl.ds(h * HD, HD)

    def w_rows(group, first, count):
        return pl.ds(pl.multiple_of(group * width + first, piece), count)

    def w_cols(group):
        return pl.ds(pl.multiple_of(group * cols, 128), cols)

    def sign(d):
        return 1 if d == 0 else -1

    def kv_copy(d, r, h):
        to = me + sign(d)
        return pltpu.make_async_remote_copy(
            src_ref=kv.at[h, :, tile_rows(d, r - 1), :],
            dst_ref=kv.at[h, :, tile_rows(d, r), :],
            send_sem=kv_send.at[d, r - 1, h],
            recv_sem=kv_recv.at[d, r - 1, h],
            device_id={"ctx": to},
            device_id_type=MESH,
        )

    def kv_arrival(d, r, h):
        here = kv.at[h, :, tile_rows(d, r), :]
        return pltpu.make_async_remote_copy(
            src_ref=here, dst_ref=here,
            send_sem=kv_send.at[d, r - 1, h],
            recv_sem=kv_recv.at[d, r - 1, h],
            device_id={"ctx": me - sign(d)},
            device_id_type=MESH,
        )

    def sends(d, r):
        if d == 0:
            return (me - (r - 1) >= 0) & (me + 1 < n_ctx)
        return (me + (r - 1) < n_ctx) & (me - 1 >= 0)

    def gets(d, r):
        return me - r >= 0 if d == 0 else me + r < n_ctx

    def kv_start(r, h):
        for d in range(2):
            @pl.when(sends(d, r))
            def _():
                kv_copy(d, r, h).start()

    def kv_wait(r, h):
        for d in range(2):
            @pl.when(gets(d, r))
            def _():
                kv_arrival(d, r, h).wait_recv()

    def bit_of(bit):
        return lax.rem(b // bit, 2)

    def partner(bit):
        return b + bit - 2 * bit * bit_of(bit)

    number = 0
    for place, bit in enumerate(bits):
        number = number + bit_of(bit) * (1 << place)

    def wy_copy(d, c):
        peer = lax.rem(mine + d, n_head)
        return pltpu.make_async_remote_copy(
            src_ref=w_out.at[
                pl.ds(pl.multiple_of(c * chunk + number * piece, piece), piece), w_cols(peer)
            ],
            dst_ref=w.at[w_rows(mine, c * chunk + number * piece, piece), :],
            send_sem=wy_send.at[d - 1, c],
            recv_sem=wy_recv.at[d - 1, c],
            device_id={"head": peer},
            device_id_type=MESH,
        )

    def wy_arrival(d, c):
        sender = lax.rem(mine + n_head - d, n_head)
        here = w.at[w_rows(sender, c * chunk + number * piece, piece), :]
        return pltpu.make_async_remote_copy(
            src_ref=here, dst_ref=here,
            send_sem=wy_send.at[d - 1, c], recv_sem=wy_recv.at[d - 1, c],
            device_id={"head": sender}, device_id_type=MESH,
        )

    def wb_copy(level, d, c, receive=False):
        sender = lax.rem(mine + n_head - d, n_head)
        block = piece << level
        index = number // (1 << level)
        if receive:
            index = index + 1 - 2 * lax.rem(index, 2)
        here = w.at[w_rows(sender, c * chunk + index * block, block), :]
        return pltpu.make_async_remote_copy(
            src_ref=here, dst_ref=here,
            send_sem=wb_send.at[level, d - 1, c], recv_sem=wb_recv.at[level, d - 1, c],
            device_id={"batch": partner(bits[level])}, device_id_type=MESH,
        )

    def w_step(stage, c):
        for d in range(1, n_head):
            if stage == 0:
                wy_arrival(d, c).wait_recv()
                if c + 1 < chunks:
                    wy_copy(d, c + 1).start()
            else:
                wb_copy(stage - 1, d, c, receive=True).wait_recv()
            if stage < len(bits):
                wb_copy(stage, d, c).start()

    def att_copy(d, h):
        return pltpu.make_async_remote_copy(
            src_ref=att.at[mine, h], dst_ref=att.at[mine, h],
            send_sem=att_send.at[d - 1, h], recv_sem=att_recv.at[d - 1, h],
            device_id={"head": lax.rem(mine + d, n_head)}, device_id_type=MESH,
        )

    def att_arrival(d, h):
        sender = lax.rem(mine + n_head - d, n_head)
        return pltpu.make_async_remote_copy(
            src_ref=att.at[sender, h], dst_ref=att.at[sender, h],
            send_sem=att_send.at[d - 1, h], recv_sem=att_recv.at[d - 1, h],
            device_id={"head": sender}, device_id_type=MESH,
        )

    def q_load():
        return pltpu.make_async_copy(queries, q, q_sem)

    def own_load(h):
        return [
            pltpu.make_async_copy(
                keyvals.at[i, :, head_cols(h)],
                kv.at[h, i // 2 + 2 * (i % 2), tile_rows(0, 0), :],
                own_sem.at[h, i],
            )
            for i in range(4)
        ]

    def own_send(h):
        for load in own_load(h):
            load.wait()
        kv_start(1, h)

    def w_load():
        return pltpu.make_async_copy(
            w_out.at[:, w_cols(mine)], w.at[w_rows(mine, 0, width), :], w_sem
        )

    barrier = pltpu.get_barrier_semaphore()
    for d in range(2):
        @pl.when(sends(d, 1))
        def _():
            pl.semaphore_signal(
                barrier, inc=1, device_id={"ctx": me + sign(d)}, device_id_type=MESH
            )
    for d in range(1, n_head):
        pl.semaphore_signal(
            barrier, inc=1, device_id={"head": lax.rem(mine + d, n_head)}, device_id_type=MESH
        )
    for bit in bits:
        pl.semaphore_signal(
            barrier, inc=1, device_id={"batch": partner(bit)}, device_id_type=MESH
        )
    q_load().start()
    for h in range(heads):
        for load in own_load(h):
            load.start()
    w_load().start()
    for d in range(2):
        @pl.when(jnp.logical_not(gets(d, 1)))
        def _():
            kv[:, :, (1 + d) * rows:(2 + d) * rows, :] = jnp.zeros(
                (heads, 4, rows, HD), jnp.bfloat16
            )
    near = jnp.where(me > 0, 1, 0) + jnp.where(me + 1 < n_ctx, 1, 0)
    pl.semaphore_wait(barrier, near + (n_head - 1 + len(bits)))

    for h in range(min(AHEAD, heads)):
        own_send(h)
    for d in range(1, n_head):
        wy_copy(d, 0).start()

    near_rows = 3 * rows
    slot_at = lax.broadcasted_iota(jnp.int32, (1, near_rows), 1) // rows
    visible = (slot_at == 0) | ((slot_at == 1) & gets(0, 1)) | ((slot_at == 2) & gets(1, 1))
    scale = 1.0 / math.sqrt(HD)

    def score(h, at):
        cols_h = slice(h * HD, (h + 1) * HD)
        q_now, q_tan = q[0, :, cols_h], q[1, :, cols_h]
        lhs = jnp.concatenate(
            [
                jnp.concatenate([q_now, jnp.zeros_like(q_now)], axis=1),
                jnp.concatenate([q_tan, q_now], axis=1),
            ],
            axis=0,
        )
        keys = jnp.concatenate([kv[h, 0, at], kv[h, 1, at]], axis=1)
        both = lax.dot_general(
            lhs, keys, (((1,), (1,)), ((), ())), preferred_element_type=jnp.float32
        )
        return both[:rows] * (scale * math.log2(math.e)), both[rows:] * scale

    def mix(h, at, expo, tan_scores):
        weighted = expo * tan_scores
        values = jnp.concatenate([kv[h, 2, at], kv[h, 3, at]], axis=1)
        left = jnp.concatenate([expo.astype(jnp.bfloat16), weighted.astype(jnp.bfloat16)], axis=0)
        mixed = jnp.dot(left, values, preferred_element_type=jnp.float32)
        return (
            jnp.sum(expo, axis=-1, keepdims=True),
            jnp.sum(weighted, axis=-1, keepdims=True),
            mixed[:rows, :HD],
            mixed[rows:, :HD] + mixed[:rows, HD:],
        )

    def attend_near(h):
        at = slice(0, near_rows)
        scores, tan_scores = score(h, at)
        scores = jnp.where(visible, scores, -jnp.inf)
        row_max = jnp.max(scores, axis=-1, keepdims=True)
        parts = mix(h, at, jnp.exp2(scores - row_max), tan_scores)
        for i, part in enumerate((row_max,) + parts):
            state[h, i] = jnp.broadcast_to(part, (rows, HD))

    def attend_far(h, d, r):
        slot = 2 * r - 1 + d
        at = slice(slot * rows, (slot + 1) * rows)
        scores, tan_scores = score(h, at)
        old_max = state[h, 0]
        row_max = jnp.maximum(old_max, jnp.max(scores, axis=-1, keepdims=True))
        shrink = jnp.exp2(old_max - row_max)
        parts = mix(h, at, jnp.exp2(scores - row_max[:, :1]), tan_scores)
        state[h, 0] = row_max
        for i, part in enumerate(parts):
            state[h, 1 + i] = state[h, 1 + i] * shrink + part

    def attend(h):
        for r in range(2, RADIUS + 1):
            for d in range(2):
                @pl.when(gets(d, r))
                def _():
                    kv_arrival(d, r, h).wait_recv()
                    attend_far(h, d, r)
        inverse = 1.0 / state[h, 1]
        attended = state[h, 3] * inverse
        tangent = state[h, 4] * inverse - (state[h, 2] * inverse) * attended
        att[mine, h, :rows] = attended.astype(jnp.bfloat16)
        att[mine, h, rows:] = tangent.astype(jnp.bfloat16)
        for d in range(1, n_head):
            att_copy(d, h).start()

    block = 512 if cols % 512 == 0 else cols

    def out_copies(i):
        at = pl.ds(i * block, block)
        return [
            pltpu.make_async_copy(rounded.at[pl.ds(n * rows, rows), at], to.at[:, at], out_sem.at[n, i])
            for n, to in enumerate((out, out_tan))
        ]

    def finish(group, first, count):
        left = jnp.concatenate([att[group, first + i] for i in range(count)], axis=1)
        for i in range(cols // block):
            at = slice(i * block, (i + 1) * block)
            part = jnp.dot(
                left, w[w_rows(group, first * HD, count * HD), at],
                preferred_element_type=jnp.float32,
            )
            rounded[:, at] = (acc[:, at] + part).astype(rounded.dtype)
            for copy in out_copies(i):
                copy.start()

    def project(group, first, count, fresh=False):
        left = jnp.concatenate([att[group, first + i] for i in range(count)], axis=1)
        part = jnp.dot(
            left, w[w_rows(group, first * HD, count * HD), :], preferred_element_type=jnp.float32
        )
        if fresh:
            acc[...] = part
        else:
            acc[...] += part

    def near_step(h):
        kv_wait(1, h)
        kv_start(2, h)
        if h + AHEAD < heads:
            own_send(h + AHEAD)

    def project_far(c):
        for d in range(1, n_head):
            for i in range(pair):
                att_arrival(d, c * pair + i).wait_recv()
            last = c == chunks - 1 and d == n_head - 1
            (finish if last else project)(lax.rem(mine + n_head - d, n_head), c * pair, pair)

    arrived = 0
    projected = 0

    def w_steps(step):
        done = 0
        for stage in range(len(bits) + 1):
            if 0 <= step - stage < chunks:
                w_step(stage, step - stage)
                done += stage == len(bits)
        return done

    q_load().wait()
    near_step(0)
    attend_near(0)
    for h in range(heads):
        if h + 1 < heads:
            near_step(h + 1)
            attend_near(h + 1)
        if h == 1:
            w_load().wait()
        if h > 0:
            arrived += w_steps(h - 1)
            if h % pair == 0:
                project(mine, h - pair, pair, fresh=h == pair)
            if projected < arrived and (projected + 1) * pair < h:
                project_far(projected)
                projected += 1
        attend(h)
    project(mine, heads - pair, pair, fresh=heads == pair)
    arrived += w_steps(heads - 1)
    for step in range(heads, chunks + len(bits)):
        arrived += w_steps(step)
    for c in range(projected, chunks):
        project_far(c)
    for h in range(heads):
        for r in range(1, RADIUS + 1):
            for d in range(2):
                @pl.when(sends(d, r))
                def _():
                    kv_copy(d, r, h).wait_send()
        for d in range(1, n_head):
            att_copy(d, h).wait_send()
    for d in range(1, n_head):
        for c in range(chunks):
            wy_copy(d, c).wait_send()
            for level in range(len(bits)):
                wb_copy(level, d, c).wait_send()
    for i in range(cols // block):
        for copy in out_copies(i):
            copy.wait()


def place(results, results_tan, out, out_tan, held, in_sem, out_sem):
    rows = out.shape[0] // PIECES
    loads, stores = [], []
    for i in range(PIECES):
        at = pl.ds(i * rows, rows)
        for n, (src, dst) in enumerate(((results, out), (results_tan, out_tan))):
            loads.append(pltpu.make_async_copy(src.at[at], held.at[n, at], in_sem.at[n, i]))
            stores.append(pltpu.make_async_copy(held.at[n, at], dst.at[at], out_sem.at[n, i]))
    for load in loads:
        load.start()
    for load, store in zip(loads, stores):
        load.wait()
        store.start()
    for store in stores:
        store.wait()


def per_device(sizes, queries, keyvals, w_out):
    n_ctx, n_head, n_batch = sizes
    rows, width = queries.shape[1], queries.shape[2]
    heads = width // HD
    cols = w_out.shape[1] // n_head
    slots = 2 * RADIUS + 1
    dma = pltpu.SemaphoreType.DMA
    peers = max(n_head - 1, 1)
    results = pl.pallas_call(
        functools.partial(kernel, sizes),
        out_shape=[jax.ShapeDtypeStruct((rows, cols), jnp.bfloat16)] * 2,
        in_specs=[pl.BlockSpec(memory_space=pl.ANY)] * 3,
        out_specs=[pl.BlockSpec(memory_space=pl.ANY)] * 2,
        scratch_shapes=[
            pltpu.VMEM((2, rows, width), jnp.bfloat16),
            pltpu.VMEM((heads, 4, slots * rows, HD), jnp.bfloat16),
            pltpu.VMEM((n_head * width, cols), jnp.bfloat16),
            pltpu.VMEM((n_head, heads, 2 * rows, HD), jnp.bfloat16),
            pltpu.VMEM((2 * rows, cols), jnp.float32),
            pltpu.VMEM((2 * rows, cols), jnp.bfloat16),
            pltpu.VMEM((heads, 5, rows, HD), jnp.float32),
            dma, dma((heads, 4)), dma((2, cols // HD)), dma,
            dma((2, RADIUS, heads)), dma((2, RADIUS, heads)),
            dma((peers, heads)), dma((peers, heads)),
            dma((peers, heads)), dma((peers, heads)),
            dma((2, peers, heads)), dma((2, peers, heads)),
        ],
        compiler_params=pltpu.CompilerParams(
            collective_id=0, has_side_effects=True, vmem_limit_bytes=63 * 1024 * 1024
        ),
        cost_estimate=pl.CostEstimate(
            flops=2 * 2 * rows * n_head * width * cols,
            bytes_accessed=16 * rows * width + 2 * w_out.size,
            transcendentals=heads * rows * slots * rows,
        ),
    )(queries, keyvals, w_out)
    return pl.pallas_call(
        place,
        out_shape=[jax.ShapeDtypeStruct((rows, cols), jnp.bfloat16)] * 2,
        in_specs=[pl.BlockSpec(memory_space=pl.ANY)] * 2,
        out_specs=[pl.BlockSpec(memory_space=pl.ANY)] * 2,
        scratch_shapes=[
            pltpu.VMEM((2, rows, cols), jnp.bfloat16), dma((2, PIECES)), dma((2, PIECES)),
        ],
        compiler_params=pltpu.CompilerParams(vmem_limit_bytes=63 * 1024 * 1024),
    )(*results)


def solution(mesh):
    sizes = (mesh.shape["ctx"], mesh.shape["head"], mesh.shape["batch"])
    in_specs = (
        P(None, ("batch", "ctx"), "head"),
        P(None, ("batch", "ctx"), "head"),
        P("head", None),
    )
    out_specs = (P(("batch", "ctx"), "head"), P(("batch", "ctx"), "head"))
    return jax.shard_map(
        functools.partial(per_device, sizes),
        mesh=mesh, in_specs=in_specs, out_specs=out_specs, check_vma=False,
    )
```

```python
import functools
import math

import jax
import jax.numpy as jnp
from jax import lax
from jax.experimental import pallas as pl
from jax.experimental.pallas import tpu as pltpu
from jax.sharding import PartitionSpec as P

HD = 128
RADIUS = 2
AHEAD = 3
LOOK = 2
PIECES = 4
MESH = pl.DeviceIdType.MESH


def kernel(
    sizes, queries, keyvals, w_out, out, out_tan,
    q, kv, w, att, acc, rounded, state,
    q_sem, own_sem, out_sem, w_sem, kv_send, kv_recv, att_send, att_recv,
    wy_send, wy_recv, wb_send, wb_recv,
):
    n_ctx, n_head, n_batch = sizes
    rows = queries.shape[1]
    width = queries.shape[2]
    heads = width // HD
    cols = out.shape[1]
    me = lax.axis_index("ctx")
    mine = lax.axis_index("head")
    b = lax.axis_index("batch")
    bits = [2, 1] if n_batch % 4 == 0 else [1] if n_batch % 2 == 0 else []
    pair = 2 if heads % 2 == 0 else 1
    chunk = pair * HD
    chunks = heads // pair
    piece = chunk // (1 << len(bits))

    def tile_rows(d, r):
        slot = 0 if r == 0 else 2 * r - 1 + d
        return pl.ds(slot * rows, rows)

    def head_cols(h):
        return pl.ds(h * HD, HD)

    def w_rows(group, first, count):
        return pl.ds(pl.multiple_of(group * width + first, piece), count)

    def w_cols(group):
        return pl.ds(pl.multiple_of(group * cols, 128), cols)

    def sign(d):
        return 1 if d == 0 else -1

    def kv_copy(d, r, h):
        to = me + sign(d)
        return pltpu.make_async_remote_copy(
            src_ref=kv.at[h, :, tile_rows(d, r - 1), :],
            dst_ref=kv.at[h, :, tile_rows(d, r), :],
            send_sem=kv_send.at[d, r - 1, h],
            recv_sem=kv_recv.at[d, r - 1, h],
            device_id={"ctx": to},
            device_id_type=MESH,
        )

    def kv_arrival(d, r, h):
        here = kv.at[h, :, tile_rows(d, r), :]
        return pltpu.make_async_remote_copy(
            src_ref=here, dst_ref=here,
            send_sem=kv_send.at[d, r - 1, h],
            recv_sem=kv_recv.at[d, r - 1, h],
            device_id={"ctx": me - sign(d)},
            device_id_type=MESH,
        )

    def sends(d, r):
        if d == 0:
            return (me - (r - 1) >= 0) & (me + 1 < n_ctx)
        return (me + (r - 1) < n_ctx) & (me - 1 >= 0)

    def gets(d, r):
        return me - r >= 0 if d == 0 else me + r < n_ctx

    def kv_start(r, h):
        for d in range(2):
            @pl.when(sends(d, r))
            def _():
                kv_copy(d, r, h).start()

    def kv_wait(r, h):
        for d in range(2):
            @pl.when(gets(d, r))
            def _():
                kv_arrival(d, r, h).wait_recv()

    def bit_of(bit):
        return lax.rem(b // bit, 2)

    def partner(bit):
        return b + bit - 2 * bit * bit_of(bit)

    number = 0
    for place, bit in enumerate(bits):
        number = number + bit_of(bit) * (1 << place)

    def wy_copy(d, c):
        peer = lax.rem(mine + d, n_head)
        return pltpu.make_async_remote_copy(
            src_ref=w_out.at[
                pl.ds(pl.multiple_of(c * chunk + number * piece, piece), piece), w_cols(peer)
            ],
            dst_ref=w.at[w_rows(mine, c * chunk + number * piece, piece), :],
            send_sem=wy_send.at[d - 1, c],
            recv_sem=wy_recv.at[d - 1, c],
            device_id={"head": peer},
            device_id_type=MESH,
        )

    def wy_arrival(d, c):
        sender = lax.rem(mine + n_head - d, n_head)
        here = w.at[w_rows(sender, c * chunk + number * piece, piece), :]
        return pltpu.make_async_remote_copy(
            src_ref=here, dst_ref=here,
            send_sem=wy_send.at[d - 1, c], recv_sem=wy_recv.at[d - 1, c],
            device_id={"head": sender}, device_id_type=MESH,
        )

    def wb_copy(level, d, c, receive=False):
        sender = lax.rem(mine + n_head - d, n_head)
        block = piece << level
        index = number // (1 << level)
        if receive:
            index = index + 1 - 2 * lax.rem(index, 2)
        here = w.at[w_rows(sender, c * chunk + index * block, block), :]
        return pltpu.make_async_remote_copy(
            src_ref=here, dst_ref=here,
            send_sem=wb_send.at[level, d - 1, c], recv_sem=wb_recv.at[level, d - 1, c],
            device_id={"batch": partner(bits[level])}, device_id_type=MESH,
        )

    def w_step(stage, c):
        for d in range(1, n_head):
            if stage == 0:
                wy_arrival(d, c).wait_recv()
                if c + 1 < chunks:
                    wy_copy(d, c + 1).start()
            else:
                wb_copy(stage - 1, d, c, receive=True).wait_recv()
            if stage < len(bits):
                wb_copy(stage, d, c).start()

    def att_copy(d, h):
        return pltpu.make_async_remote_copy(
            src_ref=att.at[mine, h], dst_ref=att.at[mine, h],
            send_sem=att_send.at[d - 1, h], recv_sem=att_recv.at[d - 1, h],
            device_id={"head": lax.rem(mine + d, n_head)}, device_id_type=MESH,
        )

    def att_arrival(d, h):
        sender = lax.rem(mine + n_head - d, n_head)
        return pltpu.make_async_remote_copy(
            src_ref=att.at[sender, h], dst_ref=att.at[sender, h],
            send_sem=att_send.at[d - 1, h], recv_sem=att_recv.at[d - 1, h],
            device_id={"head": sender}, device_id_type=MESH,
        )

    def q_load():
        return pltpu.make_async_copy(queries, q, q_sem)

    def own_load(h):
        return [
            pltpu.make_async_copy(
                keyvals.at[i, :, head_cols(h)],
                kv.at[h, i // 2 + 2 * (i % 2), tile_rows(0, 0), :],
                own_sem.at[h, i],
            )
            for i in range(4)
        ]

    def own_send(h):
        for load in own_load(h):
            load.wait()
        kv_start(1, h)

    def w_load():
        return pltpu.make_async_copy(
            w_out.at[:, w_cols(mine)], w.at[w_rows(mine, 0, width), :], w_sem
        )

    barrier = pltpu.get_barrier_semaphore()
    for d in range(2):
        @pl.when(sends(d, 1))
        def _():
            pl.semaphore_signal(
                barrier, inc=1, device_id={"ctx": me + sign(d)}, device_id_type=MESH
            )
    for d in range(1, n_head):
        pl.semaphore_signal(
            barrier, inc=1, device_id={"head": lax.rem(mine + d, n_head)}, device_id_type=MESH
        )
    for bit in bits:
        pl.semaphore_signal(
            barrier, inc=1, device_id={"batch": partner(bit)}, device_id_type=MESH
        )
    q_load().start()
    for h in range(heads):
        for load in own_load(h):
            load.start()
    w_load().start()
    for d in range(2):
        @pl.when(jnp.logical_not(gets(d, 1)))
        def _():
            kv[:, :, (1 + d) * rows:(2 + d) * rows, :] = jnp.zeros(
                (heads, 4, rows, HD), jnp.bfloat16
            )
    near = jnp.where(me > 0, 1, 0) + jnp.where(me + 1 < n_ctx, 1, 0)
    pl.semaphore_wait(barrier, near + (n_head - 1 + len(bits)))

    for h in range(min(AHEAD, heads)):
        own_send(h)
    for d in range(1, n_head):
        wy_copy(d, 0).start()

    near_rows = 3 * rows
    slot_at = lax.broadcasted_iota(jnp.int32, (1, near_rows), 1) // rows
    visible = (slot_at == 0) | ((slot_at == 1) & gets(0, 1)) | ((slot_at == 2) & gets(1, 1))
    scale = 1.0 / math.sqrt(HD)

    def score(h, at):
        cols_h = slice(h * HD, (h + 1) * HD)
        q_now, q_tan = q[0, :, cols_h], q[1, :, cols_h]
        lhs = jnp.concatenate(
            [
                jnp.concatenate([q_now, jnp.zeros_like(q_now)], axis=1),
                jnp.concatenate([q_tan, q_now], axis=1),
            ],
            axis=0,
        )
        keys = jnp.concatenate([kv[h, 0, at], kv[h, 1, at]], axis=1)
        both = lax.dot_general(
            lhs, keys, (((1,), (1,)), ((), ())), preferred_element_type=jnp.float32
        )
        return both[:rows] * (scale * math.log2(math.e)), both[rows:] * scale

    def mix(h, at, expo, tan_scores):
        weighted = expo * tan_scores
        values = jnp.concatenate([kv[h, 2, at], kv[h, 3, at]], axis=1)
        left = jnp.concatenate([expo.astype(jnp.bfloat16), weighted.astype(jnp.bfloat16)], axis=0)
        mixed = jnp.dot(left, values, preferred_element_type=jnp.float32)
        return (
            jnp.sum(expo, axis=-1, keepdims=True),
            jnp.sum(weighted, axis=-1, keepdims=True),
            mixed[:rows, :HD],
            mixed[rows:, :HD] + mixed[:rows, HD:],
        )

    def attend_near(h):
        at = slice(0, near_rows)
        scores, tan_scores = score(h, at)
        scores = jnp.where(visible, scores, -jnp.inf)
        row_max = jnp.max(scores, axis=-1, keepdims=True)
        parts = mix(h, at, jnp.exp2(scores - row_max), tan_scores)
        for i, part in enumerate((row_max,) + parts):
            state[h, i] = jnp.broadcast_to(part, (rows, HD))

    def attend_far(h, d, r):
        slot = 2 * r - 1 + d
        at = slice(slot * rows, (slot + 1) * rows)
        scores, tan_scores = score(h, at)
        old_max = state[h, 0]
        row_max = jnp.maximum(old_max, jnp.max(scores, axis=-1, keepdims=True))
        shrink = jnp.exp2(old_max - row_max)
        parts = mix(h, at, jnp.exp2(scores - row_max[:, :1]), tan_scores)
        state[h, 0] = row_max
        for i, part in enumerate(parts):
            state[h, 1 + i] = state[h, 1 + i] * shrink + part

    def attend(h):
        for r in range(2, RADIUS + 1):
            for d in range(2):
                @pl.when(gets(d, r))
                def _():
                    kv_arrival(d, r, h).wait_recv()
                    attend_far(h, d, r)
        inverse = 1.0 / state[h, 1]
        attended = state[h, 3] * inverse
        tangent = state[h, 4] * inverse - (state[h, 2] * inverse) * attended
        att[mine, h, :rows] = attended.astype(jnp.bfloat16)
        att[mine, h, rows:] = tangent.astype(jnp.bfloat16)
        for d in range(1, n_head):
            att_copy(d, h).start()

    block = 512 if cols % 512 == 0 else cols

    def out_copies(i):
        at = pl.ds(i * block, block)
        return [
            pltpu.make_async_copy(rounded.at[pl.ds(n * rows, rows), at], to.at[:, at], out_sem.at[n, i])
            for n, to in enumerate((out, out_tan))
        ]

    def finish(group, first, count):
        left = jnp.concatenate([att[group, first + i] for i in range(count)], axis=1)
        for i in range(cols // block):
            at = slice(i * block, (i + 1) * block)
            part = jnp.dot(
                left, w[w_rows(group, first * HD, count * HD), at],
                preferred_element_type=jnp.float32,
            )
            rounded[:, at] = (acc[:, at] + part).astype(rounded.dtype)
            for copy in out_copies(i):
                copy.start()

    def project(group, first, count, fresh=False):
        left = jnp.concatenate([att[group, first + i] for i in range(count)], axis=1)
        part = jnp.dot(
            left, w[w_rows(group, first * HD, count * HD), :], preferred_element_type=jnp.float32
        )
        if fresh:
            acc[...] = part
        else:
            acc[...] += part

    def near_step(h):
        kv_wait(1, h)
        kv_start(2, h)
        if h + AHEAD < heads:
            own_send(h + AHEAD)

    def project_far(c):
        for d in range(1, n_head):
            for i in range(pair):
                att_arrival(d, c * pair + i).wait_recv()
            last = c == chunks - 1 and d == n_head - 1
            (finish if last else project)(lax.rem(mine + n_head - d, n_head), c * pair, pair)

    arrived = 0
    projected = 0

    def w_steps(step):
        done = 0
        for stage in range(len(bits) + 1):
            if 0 <= step - stage < chunks:
                w_step(stage, step - stage)
                done += stage == len(bits)
        return done

    q_load().wait()
    near_step(0)
    attend_near(0)
    for h in range(1, min(LOOK, heads)):
        near_step(h)
    for h in range(heads):
        if h + LOOK < heads:
            near_step(h + LOOK)
        if h + 1 < heads:
            attend_near(h + 1)
        if h == 1:
            w_load().wait()
        if h > 0:
            arrived += w_steps(h - 1)
            if h % pair == 0:
                project(mine, h - pair, pair, fresh=h == pair)
            if projected < arrived and (projected + 1) * pair < h:
                project_far(projected)
                projected += 1
        attend(h)
    project(mine, heads - pair, pair, fresh=heads == pair)
    arrived += w_steps(heads - 1)
    for step in range(heads, chunks + len(bits)):
        arrived += w_steps(step)
    for c in range(projected, chunks):
        project_far(c)
    for h in range(heads):
        for r in range(1, RADIUS + 1):
            for d in range(2):
                @pl.when(sends(d, r))
                def _():
                    kv_copy(d, r, h).wait_send()
        for d in range(1, n_head):
            att_copy(d, h).wait_send()
    for d in range(1, n_head):
        for c in range(chunks):
            wy_copy(d, c).wait_send()
            for level in range(len(bits)):
                wb_copy(level, d, c).wait_send()
    for i in range(cols // block):
        for copy in out_copies(i):
            copy.wait()


def place(results, results_tan, out, out_tan, held, in_sem, out_sem):
    rows = out.shape[0] // PIECES
    loads, stores = [], []
    for i in range(PIECES):
        at = pl.ds(i * rows, rows)
        for n, (src, dst) in enumerate(((results, out), (results_tan, out_tan))):
            loads.append(pltpu.make_async_copy(src.at[at], held.at[n, at], in_sem.at[n, i]))
            stores.append(pltpu.make_async_copy(held.at[n, at], dst.at[at], out_sem.at[n, i]))
    for load in loads:
        load.start()
    for load, store in zip(loads, stores):
        load.wait()
        store.start()
    for store in stores:
        store.wait()


def per_device(sizes, queries, keyvals, w_out):
    n_ctx, n_head, n_batch = sizes
    rows, width = queries.shape[1], queries.shape[2]
    heads = width // HD
    cols = w_out.shape[1] // n_head
    slots = 2 * RADIUS + 1
    dma = pltpu.SemaphoreType.DMA
    peers = max(n_head - 1, 1)
    results = pl.pallas_call(
        functools.partial(kernel, sizes),
        out_shape=[jax.ShapeDtypeStruct((rows, cols), jnp.bfloat16)] * 2,
        in_specs=[pl.BlockSpec(memory_space=pl.ANY)] * 3,
        out_specs=[pl.BlockSpec(memory_space=pl.ANY)] * 2,
        scratch_shapes=[
            pltpu.VMEM((2, rows, width), jnp.bfloat16),
            pltpu.VMEM((heads, 4, slots * rows, HD), jnp.bfloat16),
            pltpu.VMEM((n_head * width, cols), jnp.bfloat16),
            pltpu.VMEM((n_head, heads, 2 * rows, HD), jnp.bfloat16),
            pltpu.VMEM((2 * rows, cols), jnp.float32),
            pltpu.VMEM((2 * rows, cols), jnp.bfloat16),
            pltpu.VMEM((heads, 5, rows, HD), jnp.float32),
            dma, dma((heads, 4)), dma((2, cols // HD)), dma,
            dma((2, RADIUS, heads)), dma((2, RADIUS, heads)),
            dma((peers, heads)), dma((peers, heads)),
            dma((peers, heads)), dma((peers, heads)),
            dma((2, peers, heads)), dma((2, peers, heads)),
        ],
        compiler_params=pltpu.CompilerParams(
            collective_id=0, has_side_effects=True, vmem_limit_bytes=63 * 1024 * 1024
        ),
        cost_estimate=pl.CostEstimate(
            flops=2 * 2 * rows * n_head * width * cols,
            bytes_accessed=16 * rows * width + 2 * w_out.size,
            transcendentals=heads * rows * slots * rows,
        ),
    )(queries, keyvals, w_out)
    return pl.pallas_call(
        place,
        out_shape=[jax.ShapeDtypeStruct((rows, cols), jnp.bfloat16)] * 2,
        in_specs=[pl.BlockSpec(memory_space=pl.ANY)] * 2,
        out_specs=[pl.BlockSpec(memory_space=pl.ANY)] * 2,
        scratch_shapes=[
            pltpu.VMEM((2, rows, cols), jnp.bfloat16), dma((2, PIECES)), dma((2, PIECES)),
        ],
        compiler_params=pltpu.CompilerParams(vmem_limit_bytes=63 * 1024 * 1024),
    )(*results)


def solution(mesh):
    sizes = (mesh.shape["ctx"], mesh.shape["head"], mesh.shape["batch"])
    in_specs = (
        P(None, ("batch", "ctx"), "head"),
        P(None, ("batch", "ctx"), "head"),
        P("head", None),
    )
    out_specs = (P(("batch", "ctx"), "head"), P(("batch", "ctx"), "head"))
    return jax.shard_map(
        functools.partial(per_device, sizes),
        mesh=mesh, in_specs=in_specs, out_specs=out_specs, check_vma=False,
    )
```

```python
import functools
import math

import jax
import jax.numpy as jnp
from jax import lax
from jax.experimental import pallas as pl
from jax.experimental.pallas import tpu as pltpu
from jax.sharding import PartitionSpec as P

HD = 128
RADIUS = 2
AHEAD = 3
LOOK = 2
PIECES = 4
MESH = pl.DeviceIdType.MESH


def kernel(
    sizes, queries, keyvals, w_out, out, out_tan,
    q, kv, w, att, acc, rounded, state,
    q_sem, own_sem, out_sem, w_sem, kv_send, kv_recv, att_send, att_recv,
    wy_send, wy_recv, wb_send, wb_recv,
):
    n_ctx, n_head, n_batch = sizes
    rows = queries.shape[1]
    width = queries.shape[2]
    heads = width // HD
    cols = out.shape[1]
    me = lax.axis_index("ctx")
    mine = lax.axis_index("head")
    b = lax.axis_index("batch")
    bits = [2, 1] if n_batch % 4 == 0 else [1] if n_batch % 2 == 0 else []
    pair = 2 if heads % 2 == 0 else 1
    chunk = pair * HD
    chunks = heads // pair
    piece = chunk // (1 << len(bits))

    def tile_rows(d, r):
        slot = 0 if r == 0 else 2 * r - 1 + d
        return pl.ds(slot * rows, rows)

    def head_cols(h):
        return pl.ds(h * HD, HD)

    def w_rows(group, first, count):
        return pl.ds(pl.multiple_of(group * width + first, piece), count)

    def w_cols(group):
        return pl.ds(pl.multiple_of(group * cols, 128), cols)

    def sign(d):
        return 1 if d == 0 else -1

    def kv_copy(d, r, h):
        to = me + sign(d)
        return pltpu.make_async_remote_copy(
            src_ref=kv.at[h, :, tile_rows(d, r - 1), :],
            dst_ref=kv.at[h, :, tile_rows(d, r), :],
            send_sem=kv_send.at[d, r - 1, h],
            recv_sem=kv_recv.at[d, r - 1, h],
            device_id={"ctx": to},
            device_id_type=MESH,
        )

    def kv_arrival(d, r, h):
        here = kv.at[h, :, tile_rows(d, r), :]
        return pltpu.make_async_remote_copy(
            src_ref=here, dst_ref=here,
            send_sem=kv_send.at[d, r - 1, h],
            recv_sem=kv_recv.at[d, r - 1, h],
            device_id={"ctx": me - sign(d)},
            device_id_type=MESH,
        )

    def sends(d, r):
        if d == 0:
            return (me - (r - 1) >= 0) & (me + 1 < n_ctx)
        return (me + (r - 1) < n_ctx) & (me - 1 >= 0)

    def gets(d, r):
        return me - r >= 0 if d == 0 else me + r < n_ctx

    def kv_start(r, h):
        for d in range(2):
            @pl.when(sends(d, r))
            def _():
                kv_copy(d, r, h).start()

    def kv_wait(r, h):
        for d in range(2):
            @pl.when(gets(d, r))
            def _():
                kv_arrival(d, r, h).wait_recv()

    def bit_of(bit):
        return lax.rem(b // bit, 2)

    def partner(bit):
        return b + bit - 2 * bit * bit_of(bit)

    number = 0
    for place, bit in enumerate(bits):
        number = number + bit_of(bit) * (1 << place)

    def wy_copy(d, c):
        peer = lax.rem(mine + d, n_head)
        return pltpu.make_async_remote_copy(
            src_ref=w_out.at[
                pl.ds(pl.multiple_of(c * chunk + number * piece, piece), piece), w_cols(peer)
            ],
            dst_ref=w.at[w_rows(mine, c * chunk + number * piece, piece), :],
            send_sem=wy_send.at[d - 1, c],
            recv_sem=wy_recv.at[d - 1, c],
            device_id={"head": peer},
            device_id_type=MESH,
        )

    def wy_arrival(d, c):
        sender = lax.rem(mine + n_head - d, n_head)
        here = w.at[w_rows(sender, c * chunk + number * piece, piece), :]
        return pltpu.make_async_remote_copy(
            src_ref=here, dst_ref=here,
            send_sem=wy_send.at[d - 1, c], recv_sem=wy_recv.at[d - 1, c],
            device_id={"head": sender}, device_id_type=MESH,
        )

    def wb_copy(level, d, c, receive=False):
        sender = lax.rem(mine + n_head - d, n_head)
        block = piece << level
        index = number // (1 << level)
        if receive:
            index = index + 1 - 2 * lax.rem(index, 2)
        here = w.at[w_rows(sender, c * chunk + index * block, block), :]
        return pltpu.make_async_remote_copy(
            src_ref=here, dst_ref=here,
            send_sem=wb_send.at[level, d - 1, c], recv_sem=wb_recv.at[level, d - 1, c],
            device_id={"batch": partner(bits[level])}, device_id_type=MESH,
        )

    def w_step(stage, c):
        for d in range(1, n_head):
            if stage == 0:
                wy_arrival(d, c).wait_recv()
                if c + 2 < chunks:
                    wy_copy(d, c + 2).start()
            else:
                wb_copy(stage - 1, d, c, receive=True).wait_recv()
            if stage < len(bits):
                wb_copy(stage, d, c).start()

    def att_copy(d, h):
        return pltpu.make_async_remote_copy(
            src_ref=att.at[mine, h], dst_ref=att.at[mine, h],
            send_sem=att_send.at[d - 1, h], recv_sem=att_recv.at[d - 1, h],
            device_id={"head": lax.rem(mine + d, n_head)}, device_id_type=MESH,
        )

    def att_arrival(d, h):
        sender = lax.rem(mine + n_head - d, n_head)
        return pltpu.make_async_remote_copy(
            src_ref=att.at[sender, h], dst_ref=att.at[sender, h],
            send_sem=att_send.at[d - 1, h], recv_sem=att_recv.at[d - 1, h],
            device_id={"head": sender}, device_id_type=MESH,
        )

    def q_load():
        return pltpu.make_async_copy(queries, q, q_sem)

    def own_load(h):
        return [
            pltpu.make_async_copy(
                keyvals.at[i, :, head_cols(h)],
                kv.at[h, i // 2 + 2 * (i % 2), tile_rows(0, 0), :],
                own_sem.at[h, i],
            )
            for i in range(4)
        ]

    def own_send(h):
        for load in own_load(h):
            load.wait()
        kv_start(1, h)

    def w_load():
        return pltpu.make_async_copy(
            w_out.at[:, w_cols(mine)], w.at[w_rows(mine, 0, width), :], w_sem
        )

    barrier = pltpu.get_barrier_semaphore()
    for d in range(2):
        @pl.when(sends(d, 1))
        def _():
            pl.semaphore_signal(
                barrier, inc=1, device_id={"ctx": me + sign(d)}, device_id_type=MESH
            )
    for d in range(1, n_head):
        pl.semaphore_signal(
            barrier, inc=1, device_id={"head": lax.rem(mine + d, n_head)}, device_id_type=MESH
        )
    for bit in bits:
        pl.semaphore_signal(
            barrier, inc=1, device_id={"batch": partner(bit)}, device_id_type=MESH
        )
    q_load().start()
    for h in range(heads):
        for load in own_load(h):
            load.start()
    w_load().start()
    for d in range(2):
        @pl.when(jnp.logical_not(gets(d, 1)))
        def _():
            kv[:, :, (1 + d) * rows:(2 + d) * rows, :] = jnp.zeros(
                (heads, 4, rows, HD), jnp.bfloat16
            )
    near = jnp.where(me > 0, 1, 0) + jnp.where(me + 1 < n_ctx, 1, 0)
    pl.semaphore_wait(barrier, near + (n_head - 1 + len(bits)))

    for h in range(min(AHEAD, heads)):
        own_send(h)
    for d in range(1, n_head):
        for c in range(min(2, chunks)):
            wy_copy(d, c).start()

    near_rows = 3 * rows
    slot_at = lax.broadcasted_iota(jnp.int32, (1, near_rows), 1) // rows
    visible = (slot_at == 0) | ((slot_at == 1) & gets(0, 1)) | ((slot_at == 2) & gets(1, 1))
    scale = 1.0 / math.sqrt(HD)

    def score(h, at):
        cols_h = slice(h * HD, (h + 1) * HD)
        q_now, q_tan = q[0, :, cols_h], q[1, :, cols_h]
        lhs = jnp.concatenate(
            [
                jnp.concatenate([q_now, jnp.zeros_like(q_now)], axis=1),
                jnp.concatenate([q_tan, q_now], axis=1),
            ],
            axis=0,
        )
        keys = jnp.concatenate([kv[h, 0, at], kv[h, 1, at]], axis=1)
        both = lax.dot_general(
            lhs, keys, (((1,), (1,)), ((), ())), preferred_element_type=jnp.float32
        )
        return both[:rows] * (scale * math.log2(math.e)), both[rows:] * scale

    def mix(h, at, expo, tan_scores):
        weighted = expo * tan_scores
        values = jnp.concatenate([kv[h, 2, at], kv[h, 3, at]], axis=1)
        left = jnp.concatenate([expo.astype(jnp.bfloat16), weighted.astype(jnp.bfloat16)], axis=0)
        mixed = jnp.dot(left, values, preferred_element_type=jnp.float32)
        return (
            jnp.sum(expo, axis=-1, keepdims=True),
            jnp.sum(weighted, axis=-1, keepdims=True),
            mixed[:rows, :HD],
            mixed[rows:, :HD] + mixed[:rows, HD:],
        )

    def attend_near(h):
        at = slice(0, near_rows)
        scores, tan_scores = score(h, at)
        scores = jnp.where(visible, scores, -jnp.inf)
        row_max = jnp.max(scores, axis=-1, keepdims=True)
        parts = mix(h, at, jnp.exp2(scores - row_max), tan_scores)
        for i, part in enumerate((row_max,) + parts):
            state[h, i] = jnp.broadcast_to(part, (rows, HD))

    def attend_far(h, d, r):
        slot = 2 * r - 1 + d
        at = slice(slot * rows, (slot + 1) * rows)
        scores, tan_scores = score(h, at)
        old_max = state[h, 0]
        row_max = jnp.maximum(old_max, jnp.max(scores, axis=-1, keepdims=True))
        shrink = jnp.exp2(old_max - row_max)
        parts = mix(h, at, jnp.exp2(scores - row_max[:, :1]), tan_scores)
        state[h, 0] = row_max
        for i, part in enumerate(parts):
            state[h, 1 + i] = state[h, 1 + i] * shrink + part

    def attend(h):
        for r in range(2, RADIUS + 1):
            for d in range(2):
                @pl.when(gets(d, r))
                def _():
                    kv_arrival(d, r, h).wait_recv()
                    attend_far(h, d, r)
        inverse = 1.0 / state[h, 1]
        attended = state[h, 3] * inverse
        tangent = state[h, 4] * inverse - (state[h, 2] * inverse) * attended
        att[mine, h, :rows] = attended.astype(jnp.bfloat16)
        att[mine, h, rows:] = tangent.astype(jnp.bfloat16)
        for d in range(1, n_head):
            att_copy(d, h).start()

    block = 512 if cols % 512 == 0 else cols

    def out_copies(i):
        at = pl.ds(i * block, block)
        return [
            pltpu.make_async_copy(rounded.at[pl.ds(n * rows, rows), at], to.at[:, at], out_sem.at[n, i])
            for n, to in enumerate((out, out_tan))
        ]

    def finish(group, first, count):
        left = jnp.concatenate([att[group, first + i] for i in range(count)], axis=1)
        for i in range(cols // block):
            at = slice(i * block, (i + 1) * block)
            part = jnp.dot(
                left, w[w_rows(group, first * HD, count * HD), at],
                preferred_element_type=jnp.float32,
            )
            rounded[:, at] = (acc[:, at] + part).astype(rounded.dtype)
            for copy in out_copies(i):
                copy.start()

    def project(group, first, count, fresh=False):
        left = jnp.concatenate([att[group, first + i] for i in range(count)], axis=1)
        part = jnp.dot(
            left, w[w_rows(group, first * HD, count * HD), :], preferred_element_type=jnp.float32
        )
        if fresh:
            acc[...] = part
        else:
            acc[...] += part

    def near_step(h):
        kv_wait(1, h)
        kv_start(2, h)
        if h + AHEAD < heads:
            own_send(h + AHEAD)

    def project_far(c):
        for d in range(1, n_head):
            for i in range(pair):
                att_arrival(d, c * pair + i).wait_recv()
            last = c == chunks - 1 and d == n_head - 1
            (finish if last else project)(lax.rem(mine + n_head - d, n_head), c * pair, pair)

    arrived = 0
    projected = 0

    def w_steps(step):
        done = 0
        for stage in range(len(bits) + 1):
            c = step - stage - (stage > 0)
            if 0 <= c < chunks:
                w_step(stage, c)
                done += stage == len(bits)
        return done

    q_load().wait()
    near_step(0)
    attend_near(0)
    for h in range(1, min(LOOK, heads)):
        near_step(h)
    for h in range(heads):
        if h + LOOK < heads:
            near_step(h + LOOK)
        if h + 1 < heads:
            attend_near(h + 1)
        if h == 1:
            w_load().wait()
        arrived += w_steps(h)
        if h > 0:
            if h % pair == 0:
                project(mine, h - pair, pair, fresh=h == pair)
            if projected < arrived and (projected + 1) * pair < h:
                project_far(projected)
                projected += 1
        attend(h)
    project(mine, heads - pair, pair, fresh=heads == pair)
    for step in range(heads, chunks + len(bits) + 1):
        arrived += w_steps(step)
    for c in range(projected, chunks):
        project_far(c)
    for h in range(heads):
        for r in range(1, RADIUS + 1):
            for d in range(2):
                @pl.when(sends(d, r))
                def _():
                    kv_copy(d, r, h).wait_send()
        for d in range(1, n_head):
            att_copy(d, h).wait_send()
    for d in range(1, n_head):
        for c in range(chunks):
            wy_copy(d, c).wait_send()
            for level in range(len(bits)):
                wb_copy(level, d, c).wait_send()
    for i in range(cols // block):
        for copy in out_copies(i):
            copy.wait()


def place(results, results_tan, out, out_tan, held, in_sem, out_sem):
    rows = out.shape[0] // PIECES
    loads, stores = [], []
    for i in range(PIECES):
        at = pl.ds(i * rows, rows)
        for n, (src, dst) in enumerate(((results, out), (results_tan, out_tan))):
            loads.append(pltpu.make_async_copy(src.at[at], held.at[n, at], in_sem.at[n, i]))
            stores.append(pltpu.make_async_copy(held.at[n, at], dst.at[at], out_sem.at[n, i]))
    for load in loads:
        load.start()
    for load, store in zip(loads, stores):
        load.wait()
        store.start()
    for store in stores:
        store.wait()


def per_device(sizes, queries, keyvals, w_out):
    n_ctx, n_head, n_batch = sizes
    rows, width = queries.shape[1], queries.shape[2]
    heads = width // HD
    cols = w_out.shape[1] // n_head
    slots = 2 * RADIUS + 1
    dma = pltpu.SemaphoreType.DMA
    peers = max(n_head - 1, 1)
    results = pl.pallas_call(
        functools.partial(kernel, sizes),
        out_shape=[jax.ShapeDtypeStruct((rows, cols), jnp.bfloat16)] * 2,
        in_specs=[pl.BlockSpec(memory_space=pl.ANY)] * 3,
        out_specs=[pl.BlockSpec(memory_space=pl.ANY)] * 2,
        scratch_shapes=[
            pltpu.VMEM((2, rows, width), jnp.bfloat16),
            pltpu.VMEM((heads, 4, slots * rows, HD), jnp.bfloat16),
            pltpu.VMEM((n_head * width, cols), jnp.bfloat16),
            pltpu.VMEM((n_head, heads, 2 * rows, HD), jnp.bfloat16),
            pltpu.VMEM((2 * rows, cols), jnp.float32),
            pltpu.VMEM((2 * rows, cols), jnp.bfloat16),
            pltpu.VMEM((heads, 5, rows, HD), jnp.float32),
            dma, dma((heads, 4)), dma((2, cols // HD)), dma,
            dma((2, RADIUS, heads)), dma((2, RADIUS, heads)),
            dma((peers, heads)), dma((peers, heads)),
            dma((peers, heads)), dma((peers, heads)),
            dma((2, peers, heads)), dma((2, peers, heads)),
        ],
        compiler_params=pltpu.CompilerParams(
            collective_id=0, has_side_effects=True, vmem_limit_bytes=63 * 1024 * 1024
        ),
        cost_estimate=pl.CostEstimate(
            flops=2 * 2 * rows * n_head * width * cols,
            bytes_accessed=16 * rows * width + 2 * w_out.size,
            transcendentals=heads * rows * slots * rows,
        ),
    )(queries, keyvals, w_out)
    return pl.pallas_call(
        place,
        out_shape=[jax.ShapeDtypeStruct((rows, cols), jnp.bfloat16)] * 2,
        in_specs=[pl.BlockSpec(memory_space=pl.ANY)] * 2,
        out_specs=[pl.BlockSpec(memory_space=pl.ANY)] * 2,
        scratch_shapes=[
            pltpu.VMEM((2, rows, cols), jnp.bfloat16), dma((2, PIECES)), dma((2, PIECES)),
        ],
        compiler_params=pltpu.CompilerParams(vmem_limit_bytes=63 * 1024 * 1024),
    )(*results)


def solution(mesh):
    sizes = (mesh.shape["ctx"], mesh.shape["head"], mesh.shape["batch"])
    in_specs = (
        P(None, ("batch", "ctx"), "head"),
        P(None, ("batch", "ctx"), "head"),
        P("head", None),
    )
    out_specs = (P(("batch", "ctx"), "head"), P(("batch", "ctx"), "head"))
    return jax.shard_map(
        functools.partial(per_device, sizes),
        mesh=mesh, in_specs=in_specs, out_specs=out_specs, check_vma=False,
    )
```

```python
import functools
import math

import jax
import jax.numpy as jnp
from jax import lax
from jax.experimental import pallas as pl
from jax.experimental.pallas import tpu as pltpu
from jax.sharding import PartitionSpec as P

HD = 128
RADIUS = 2
AHEAD = 2
LOOK = 2
PIECES = 4
MESH = pl.DeviceIdType.MESH


def kernel(
    sizes, queries, keyvals, w_out, out, out_tan,
    q, kv, w, att, acc, rounded, state,
    q_sem, own_sem, out_sem, w_sem, kv_send, kv_recv, att_send, att_recv,
    wy_send, wy_recv, wb_send, wb_recv,
):
    n_ctx, n_head, n_batch = sizes
    rows = queries.shape[1]
    width = queries.shape[2]
    heads = width // HD
    cols = out.shape[1]
    me = lax.axis_index("ctx")
    mine = lax.axis_index("head")
    b = lax.axis_index("batch")
    bits = [2, 1] if n_batch % 4 == 0 else [1] if n_batch % 2 == 0 else []
    pair = 2 if heads % 2 == 0 else 1
    chunk = pair * HD
    chunks = heads // pair
    piece = chunk // (1 << len(bits))

    def tile_rows(d, r):
        slot = 0 if r == 0 else 2 * r - 1 + d
        return pl.ds(slot * rows, rows)

    def head_cols(h):
        return pl.ds(h * HD, HD)

    def w_rows(group, first, count):
        return pl.ds(pl.multiple_of(group * width + first, piece), count)

    def w_cols(group):
        return pl.ds(pl.multiple_of(group * cols, 128), cols)

    def sign(d):
        return 1 if d == 0 else -1

    def kv_copy(d, r, h):
        to = me + sign(d)
        return pltpu.make_async_remote_copy(
            src_ref=kv.at[h, :, tile_rows(d, r - 1), :],
            dst_ref=kv.at[h, :, tile_rows(d, r), :],
            send_sem=kv_send.at[d, r - 1, h],
            recv_sem=kv_recv.at[d, r - 1, h],
            device_id={"ctx": to},
            device_id_type=MESH,
        )

    def kv_arrival(d, r, h):
        here = kv.at[h, :, tile_rows(d, r), :]
        return pltpu.make_async_remote_copy(
            src_ref=here, dst_ref=here,
            send_sem=kv_send.at[d, r - 1, h],
            recv_sem=kv_recv.at[d, r - 1, h],
            device_id={"ctx": me - sign(d)},
            device_id_type=MESH,
        )

    def sends(d, r):
        if d == 0:
            return (me - (r - 1) >= 0) & (me + 1 < n_ctx)
        return (me + (r - 1) < n_ctx) & (me - 1 >= 0)

    def gets(d, r):
        return me - r >= 0 if d == 0 else me + r < n_ctx

    def kv_start(r, h):
        for d in range(2):
            @pl.when(sends(d, r))
            def _():
                kv_copy(d, r, h).start()

    def kv_sent(r, h):
        for d in range(2):
            @pl.when(sends(d, r))
            def _():
                kv_copy(d, r, h).wait_send()

    def kv_wait(r, h):
        for d in range(2):
            @pl.when(gets(d, r))
            def _():
                kv_arrival(d, r, h).wait_recv()

    def bit_of(bit):
        return lax.rem(b // bit, 2)

    def partner(bit):
        return b + bit - 2 * bit * bit_of(bit)

    number = 0
    for place, bit in enumerate(bits):
        number = number + bit_of(bit) * (1 << place)

    def wy_copy(d, c):
        peer = lax.rem(mine + d, n_head)
        return pltpu.make_async_remote_copy(
            src_ref=w_out.at[
                pl.ds(pl.multiple_of(c * chunk + number * piece, piece), piece), w_cols(peer)
            ],
            dst_ref=w.at[w_rows(mine, c * chunk + number * piece, piece), :],
            send_sem=wy_send.at[d - 1, c],
            recv_sem=wy_recv.at[d - 1, c],
            device_id={"head": peer},
            device_id_type=MESH,
        )

    def wy_arrival(d, c):
        sender = lax.rem(mine + n_head - d, n_head)
        here = w.at[w_rows(sender, c * chunk + number * piece, piece), :]
        return pltpu.make_async_remote_copy(
            src_ref=here, dst_ref=here,
            send_sem=wy_send.at[d - 1, c], recv_sem=wy_recv.at[d - 1, c],
            device_id={"head": sender}, device_id_type=MESH,
        )

    def wb_copy(level, d, c, receive=False):
        sender = lax.rem(mine + n_head - d, n_head)
        block = piece << level
        index = number // (1 << level)
        if receive:
            index = index + 1 - 2 * lax.rem(index, 2)
        here = w.at[w_rows(sender, c * chunk + index * block, block), :]
        return pltpu.make_async_remote_copy(
            src_ref=here, dst_ref=here,
            send_sem=wb_send.at[level, d - 1, c], recv_sem=wb_recv.at[level, d - 1, c],
            device_id={"batch": partner(bits[level])}, device_id_type=MESH,
        )

    def w_step(stage, c):
        for d in range(1, n_head):
            if stage == 0:
                wy_arrival(d, c).wait_recv()
                if c + 2 < chunks:
                    wy_copy(d, c + 2).start()
            else:
                wb_copy(stage - 1, d, c, receive=True).wait_recv()
            if stage < len(bits):
                wb_copy(stage, d, c).start()

    def att_copy(d, h):
        return pltpu.make_async_remote_copy(
            src_ref=att.at[mine, h], dst_ref=att.at[mine, h],
            send_sem=att_send.at[d - 1, h], recv_sem=att_recv.at[d - 1, h],
            device_id={"head": lax.rem(mine + d, n_head)}, device_id_type=MESH,
        )

    def att_arrival(d, h):
        sender = lax.rem(mine + n_head - d, n_head)
        return pltpu.make_async_remote_copy(
            src_ref=att.at[sender, h], dst_ref=att.at[sender, h],
            send_sem=att_send.at[d - 1, h], recv_sem=att_recv.at[d - 1, h],
            device_id={"head": sender}, device_id_type=MESH,
        )

    def q_load():
        return pltpu.make_async_copy(queries, q, q_sem)

    def own_load(h):
        return [
            pltpu.make_async_copy(
                keyvals.at[i, :, head_cols(h)],
                kv.at[h, i // 2 + 2 * (i % 2), tile_rows(0, 0), :],
                own_sem.at[h, i],
            )
            for i in range(4)
        ]

    def own_send(h):
        for load in own_load(h):
            load.wait()
        kv_start(1, h)

    def w_load():
        return pltpu.make_async_copy(
            w_out.at[:, w_cols(mine)], w.at[w_rows(mine, 0, width), :], w_sem
        )

    barrier = pltpu.get_barrier_semaphore()
    for d in range(2):
        @pl.when(sends(d, 1))
        def _():
            pl.semaphore_signal(
                barrier, inc=1, device_id={"ctx": me + sign(d)}, device_id_type=MESH
            )
    for d in range(1, n_head):
        pl.semaphore_signal(
            barrier, inc=1, device_id={"head": lax.rem(mine + d, n_head)}, device_id_type=MESH
        )
    for bit in bits:
        pl.semaphore_signal(
            barrier, inc=1, device_id={"batch": partner(bit)}, device_id_type=MESH
        )
    q_load().start()
    for h in range(heads):
        for load in own_load(h):
            load.start()
    w_load().start()
    for d in range(2):
        @pl.when(jnp.logical_not(gets(d, 1)))
        def _():
            kv[:, :, (1 + d) * rows:(2 + d) * rows, :] = jnp.zeros(
                (heads, 4, rows, HD), jnp.bfloat16
            )
    near = jnp.where(me > 0, 1, 0) + jnp.where(me + 1 < n_ctx, 1, 0)
    pl.semaphore_wait(barrier, near + (n_head - 1 + len(bits)))

    for h in range(min(AHEAD, heads)):
        own_send(h)
    for d in range(1, n_head):
        for c in range(min(2, chunks)):
            wy_copy(d, c).start()

    near_rows = 3 * rows
    slot_at = lax.broadcasted_iota(jnp.int32, (1, near_rows), 1) // rows
    visible = (slot_at == 0) | ((slot_at == 1) & gets(0, 1)) | ((slot_at == 2) & gets(1, 1))
    scale = 1.0 / math.sqrt(HD)

    def score(h, at):
        cols_h = slice(h * HD, (h + 1) * HD)
        q_now, q_tan = q[0, :, cols_h], q[1, :, cols_h]
        lhs = jnp.concatenate(
            [
                jnp.concatenate([q_now, jnp.zeros_like(q_now)], axis=1),
                jnp.concatenate([q_tan, q_now], axis=1),
            ],
            axis=0,
        )
        keys = jnp.concatenate([kv[h, 0, at], kv[h, 1, at]], axis=1)
        both = lax.dot_general(
            lhs, keys, (((1,), (1,)), ((), ())), preferred_element_type=jnp.float32
        )
        return both[:rows] * (scale * math.log2(math.e)), both[rows:] * scale

    def mix(h, at, expo, tan_scores):
        weighted = expo * tan_scores
        values = jnp.concatenate([kv[h, 2, at], kv[h, 3, at]], axis=1)
        left = jnp.concatenate([expo.astype(jnp.bfloat16), weighted.astype(jnp.bfloat16)], axis=0)
        mixed = jnp.dot(left, values, preferred_element_type=jnp.float32)
        return (
            jnp.sum(expo, axis=-1, keepdims=True),
            jnp.sum(weighted, axis=-1, keepdims=True),
            mixed[:rows, :HD],
            mixed[rows:, :HD] + mixed[:rows, HD:],
        )

    def attend_near(h):
        at = slice(0, near_rows)
        scores, tan_scores = score(h, at)
        scores = jnp.where(visible, scores, -jnp.inf)
        row_max = jnp.max(scores, axis=-1, keepdims=True)
        parts = mix(h, at, jnp.exp2(scores - row_max), tan_scores)
        for i, part in enumerate((row_max,) + parts):
            state[h, i] = jnp.broadcast_to(part, (rows, HD))

    def attend_far(h, d, r):
        slot = 2 * r - 1 + d
        at = slice(slot * rows, (slot + 1) * rows)
        scores, tan_scores = score(h, at)
        old_max = state[h, 0]
        row_max = jnp.maximum(old_max, jnp.max(scores, axis=-1, keepdims=True))
        shrink = jnp.exp2(old_max - row_max)
        parts = mix(h, at, jnp.exp2(scores - row_max[:, :1]), tan_scores)
        state[h, 0] = row_max
        for i, part in enumerate(parts):
            state[h, 1 + i] = state[h, 1 + i] * shrink + part

    def attend(h):
        for r in range(2, RADIUS + 1):
            for d in range(2):
                @pl.when(gets(d, r))
                def _():
                    kv_arrival(d, r, h).wait_recv()
                    attend_far(h, d, r)
        inverse = 1.0 / state[h, 1]
        attended = state[h, 3] * inverse
        tangent = state[h, 4] * inverse - (state[h, 2] * inverse) * attended
        att[mine, h, :rows] = attended.astype(jnp.bfloat16)
        att[mine, h, rows:] = tangent.astype(jnp.bfloat16)
        for d in range(1, n_head):
            att_copy(d, h).start()

    block = 512 if cols % 512 == 0 else cols

    def out_copies(i):
        at = pl.ds(i * block, block)
        return [
            pltpu.make_async_copy(rounded.at[pl.ds(n * rows, rows), at], to.at[:, at], out_sem.at[n, i])
            for n, to in enumerate((out, out_tan))
        ]

    def finish(group, first, count):
        left = jnp.concatenate([att[group, first + i] for i in range(count)], axis=1)
        for i in range(cols // block):
            at = slice(i * block, (i + 1) * block)
            part = jnp.dot(
                left, w[w_rows(group, first * HD, count * HD), at],
                preferred_element_type=jnp.float32,
            )
            rounded[:, at] = (acc[:, at] + part).astype(rounded.dtype)
            for copy in out_copies(i):
                copy.start()

    def project(group, first, count, fresh=False):
        left = jnp.concatenate([att[group, first + i] for i in range(count)], axis=1)
        part = jnp.dot(
            left, w[w_rows(group, first * HD, count * HD), :], preferred_element_type=jnp.float32
        )
        if fresh:
            acc[...] = part
        else:
            acc[...] += part

    def near_step(h):
        if h + AHEAD < heads:
            kv_sent(1, h)
            own_send(h + AHEAD)
        kv_wait(1, h)
        kv_start(2, h)

    def project_far(c):
        for d in range(1, n_head):
            for i in range(pair):
                att_arrival(d, c * pair + i).wait_recv()
            last = c == chunks - 1 and d == n_head - 1
            (finish if last else project)(lax.rem(mine + n_head - d, n_head), c * pair, pair)

    arrived = 0
    projected = 0

    def w_steps(step):
        done = 0
        for stage in range(len(bits) + 1):
            c = step - stage - (stage > 0)
            if 0 <= c < chunks:
                w_step(stage, c)
                done += stage == len(bits)
        return done

    q_load().wait()
    near_step(0)
    attend_near(0)
    for h in range(1, min(LOOK, heads)):
        near_step(h)
    for h in range(heads):
        if h + LOOK < heads:
            near_step(h + LOOK)
        if h + 1 < heads:
            attend_near(h + 1)
        if h == 1:
            w_load().wait()
        arrived += w_steps(h)
        if h > 0:
            if h % pair == 0:
                project(mine, h - pair, pair, fresh=h == pair)
            if projected < arrived and (projected + 1) * pair < h:
                project_far(projected)
                projected += 1
        attend(h)
    project(mine, heads - pair, pair, fresh=heads == pair)
    for step in range(heads, chunks + len(bits) + 1):
        arrived += w_steps(step)
    for c in range(projected, chunks):
        project_far(c)
    for h in range(heads):
        for r in range(1, RADIUS + 1):
            if r > 1 or h + AHEAD >= heads:
                kv_sent(r, h)
        for d in range(1, n_head):
            att_copy(d, h).wait_send()
    for d in range(1, n_head):
        for c in range(chunks):
            wy_copy(d, c).wait_send()
            for level in range(len(bits)):
                wb_copy(level, d, c).wait_send()
    for i in range(cols // block):
        for copy in out_copies(i):
            copy.wait()


def place(results, results_tan, out, out_tan, held, in_sem, out_sem):
    rows = out.shape[0] // PIECES
    loads, stores = [], []
    for i in range(PIECES):
        at = pl.ds(i * rows, rows)
        for n, (src, dst) in enumerate(((results, out), (results_tan, out_tan))):
            loads.append(pltpu.make_async_copy(src.at[at], held.at[n, at], in_sem.at[n, i]))
            stores.append(pltpu.make_async_copy(held.at[n, at], dst.at[at], out_sem.at[n, i]))
    for load in loads:
        load.start()
    for load, store in zip(loads, stores):
        load.wait()
        store.start()
    for store in stores:
        store.wait()


def per_device(sizes, queries, keyvals, w_out):
    n_ctx, n_head, n_batch = sizes
    rows, width = queries.shape[1], queries.shape[2]
    heads = width // HD
    cols = w_out.shape[1] // n_head
    slots = 2 * RADIUS + 1
    dma = pltpu.SemaphoreType.DMA
    peers = max(n_head - 1, 1)
    results = pl.pallas_call(
        functools.partial(kernel, sizes),
        out_shape=[jax.ShapeDtypeStruct((rows, cols), jnp.bfloat16)] * 2,
        in_specs=[pl.BlockSpec(memory_space=pl.ANY)] * 3,
        out_specs=[pl.BlockSpec(memory_space=pl.ANY)] * 2,
        scratch_shapes=[
            pltpu.VMEM((2, rows, width), jnp.bfloat16),
            pltpu.VMEM((heads, 4, slots * rows, HD), jnp.bfloat16),
            pltpu.VMEM((n_head * width, cols), jnp.bfloat16),
            pltpu.VMEM((n_head, heads, 2 * rows, HD), jnp.bfloat16),
            pltpu.VMEM((2 * rows, cols), jnp.float32),
            pltpu.VMEM((2 * rows, cols), jnp.bfloat16),
            pltpu.VMEM((heads, 5, rows, HD), jnp.float32),
            dma, dma((heads, 4)), dma((2, cols // HD)), dma,
            dma((2, RADIUS, heads)), dma((2, RADIUS, heads)),
            dma((peers, heads)), dma((peers, heads)),
            dma((peers, heads)), dma((peers, heads)),
            dma((2, peers, heads)), dma((2, peers, heads)),
        ],
        compiler_params=pltpu.CompilerParams(
            collective_id=0, has_side_effects=True, vmem_limit_bytes=63 * 1024 * 1024
        ),
        cost_estimate=pl.CostEstimate(
            flops=2 * 2 * rows * n_head * width * cols,
            bytes_accessed=16 * rows * width + 2 * w_out.size,
            transcendentals=heads * rows * slots * rows,
        ),
    )(queries, keyvals, w_out)
    return pl.pallas_call(
        place,
        out_shape=[jax.ShapeDtypeStruct((rows, cols), jnp.bfloat16)] * 2,
        in_specs=[pl.BlockSpec(memory_space=pl.ANY)] * 2,
        out_specs=[pl.BlockSpec(memory_space=pl.ANY)] * 2,
        scratch_shapes=[
            pltpu.VMEM((2, rows, cols), jnp.bfloat16), dma((2, PIECES)), dma((2, PIECES)),
        ],
        compiler_params=pltpu.CompilerParams(vmem_limit_bytes=63 * 1024 * 1024),
    )(*results)


def solution(mesh):
    sizes = (mesh.shape["ctx"], mesh.shape["head"], mesh.shape["batch"])
    in_specs = (
        P(None, ("batch", "ctx"), "head"),
        P(None, ("batch", "ctx"), "head"),
        P("head", None),
    )
    out_specs = (P(("batch", "ctx"), "head"), P(("batch", "ctx"), "head"))
    return jax.shard_map(
        functools.partial(per_device, sizes),
        mesh=mesh, in_specs=in_specs, out_specs=out_specs, check_vma=False,
    )
```
